32 devices in a mesh: grp: 4 (over y, core), wsh: 8 (over z, x).
Axes of the slice: x: 2, y: 2, z: 4, core: 2. Of those that a mesh axis runs over, the one named last changes fastest.
Arguments:
- tokens: bfloat16 [2048, 2048], P('grp', 'wsh'), may hold values from -6 to 6
- gate_weight: bfloat16 [2048, 7168], P(None, 'wsh'), may hold values from -0.125 to 0.125
- up_weight: bfloat16 [2048, 7168], P(None, 'wsh'), may hold values from -0.125 to 0.125
- down_weight: bfloat16 [7168, 2048], P('wsh'), may hold values from -0.0625 to 0.0625
- gate_left: bfloat16 [256, 2048], P('grp'), may hold values from -0.125 to 0.125
- gate_right: float32 [256, 7168], P('grp', 'wsh'), may hold values from -6 to 6
- up_left: bfloat16 [256, 2048], P('grp'), may hold values from -0.125 to 0.125
- up_right: float32 [256, 7168], P('grp', 'wsh'), may hold values from -6 to 6
- down_left: bfloat16 [256, 7168], P('grp', 'wsh'), may hold values from -0.0625 to 0.0625
- down_right: float32 [256, 2048], P('grp'), may hold values from -6 to 6
- fitness_rank: int32 [256], P('grp'), may hold values from 0 to 255, each once
Outputs:
- mixed: bfloat16 [2048, 2048], P('grp', 'wsh')
- gate_step: bfloat16 [2048, 7168], P('grp', 'wsh')
- up_step: bfloat16 [2048, 7168], P('grp', 'wsh')
The draws below stay inside these ranges and needn't reach their ends.
All inputs are finite; a program needn't handle non-finite values.
Results may differ from the reference program's by a relative error of at most 0.005.
Values may be sent and summed in bfloat16 or wider, within the bound.
No kernel may reach another device: no remote copies, remote signals or barrier semaphores. Data moves between devices by JAX's collectives and lax.ppermute only.
A program may use at most 64 MiB of HBM per device.

```python
import jax
import jax.numpy as jnp
from jax import lax

D = 2048
FF = 7168
TOK_MEM = 8
MEM_GRP = 64
MEMBERS = 256
TOKENS = 2048
N_GRP = 4


def block_scale(rng, extent, cuts, low, high):
    factor_of, own = 1.0, jax.random.fold_in(rng, 6)
    for position, parts in cuts:
        heights = jnp.exp(jax.random.uniform(jax.random.fold_in(own, position), (parts,), jnp.float32, low / len(cuts), high / len(cuts)))
        factor_of = factor_of * jnp.repeat(heights, extent[position] // parts).reshape([-1 if axis == position else 1 for axis in range(len(extent))])
    return factor_of


def normal_values(key, shape, width, limit, cuts=(), kind=jnp.bfloat16):
    entries = width * jax.random.normal(key, shape, jnp.float32)
    if cuts:
        entries = entries * block_scale(key, shape, cuts, -0.22, 0.18)
    return jnp.clip(entries, -limit, limit).astype(kind)


def setup_inputs(seed: int = 0) -> dict:
    streams_of = jax.random.split(jax.random.key(seed), 12)
    return {
        "tokens": normal_values(streams_of[0], (TOKENS, D), 1.0, 6.0, ((0, 4), (1, 8))),
        "gate_weight": normal_values(streams_of[1], (D, FF), D ** -0.5, 0.125, ((1, 8),)),
        "up_weight": normal_values(streams_of[2], (D, FF), D ** -0.5, 0.125, ((1, 8),)),
        "down_weight": normal_values(streams_of[3], (FF, D), FF ** -0.5, 0.0625, ((0, 8),)),
        "gate_left": normal_values(streams_of[4], (MEMBERS, D), D ** -0.5, 0.125, ((0, 4),)),
        "gate_right": normal_values(streams_of[5], (MEMBERS, FF), 1.0, 6.0, ((0, 4), (1, 8)), jnp.float32),
        "up_left": normal_values(streams_of[6], (MEMBERS, D), D ** -0.5, 0.125, ((0, 4),)),
        "up_right": normal_values(streams_of[7], (MEMBERS, FF), 1.0, 6.0, ((0, 4), (1, 8)), jnp.float32),
        "down_left": normal_values(streams_of[8], (MEMBERS, FF), FF ** -0.5, 0.0625, ((0, 4), (1, 8))),
        "down_right": normal_values(streams_of[9], (MEMBERS, D), 1.0, 6.0, ((0, 4),), jnp.float32),
        "fitness_rank": jax.random.permutation(streams_of[10], MEMBERS).astype(jnp.int32),
    }


noise_scale = 0.5


def silu(value):
    return value / (1.0 + jnp.exp(-value))


def reference(tokens, gate_weight, up_weight, down_weight, gate_left, gate_right, up_left, up_right, down_left, down_right, fitness_rank):
    gate_full = gate_weight.astype(jnp.float32)
    up_full = up_weight.astype(jnp.float32)
    down_full = down_weight.astype(jnp.float32)
    rows = MEM_GRP * TOK_MEM

    def evaluate(pieces):
        block_tok, g_left, g_right, u_left, u_right, d_left, d_right = pieces
        tok_f = block_tok.astype(jnp.float32)
        grouped = tok_f.reshape(MEM_GRP, TOK_MEM, D)
        g_score = jnp.einsum("mtd,md->mt", grouped, g_left.astype(jnp.float32))
        u_score = jnp.einsum("mtd,md->mt", grouped, u_left.astype(jnp.float32))
        gate = jnp.dot(tok_f, gate_full, preferred_element_type=jnp.float32)
        gate = gate + noise_scale * (g_score[:, :, None] * g_right[:, None, :]).reshape(rows, FF)
        up = jnp.dot(tok_f, up_full, preferred_element_type=jnp.float32)
        up = up + noise_scale * (u_score[:, :, None] * u_right[:, None, :]).reshape(rows, FF)
        hidden = (silu(gate) * up).astype(jnp.bfloat16)
        hid_f = hidden.astype(jnp.float32)
        d_score = jnp.einsum("mtf,mf->mt", hid_f.reshape(MEM_GRP, TOK_MEM, FF), d_left.astype(jnp.float32))
        output = jnp.dot(hid_f, down_full, preferred_element_type=jnp.float32)
        output = output + noise_scale * (d_score[:, :, None] * d_right[:, None, :]).reshape(rows, D)
        return output.astype(jnp.bfloat16)

    pieces = (tokens.reshape(N_GRP, rows, D),
              gate_left.reshape(N_GRP, MEM_GRP, D), gate_right.reshape(N_GRP, MEM_GRP, FF),
              up_left.reshape(N_GRP, MEM_GRP, D), up_right.reshape(N_GRP, MEM_GRP, FF),
              down_left.reshape(N_GRP, MEM_GRP, FF), down_right.reshape(N_GRP, MEM_GRP, D))
    mixed = lax.map(evaluate, pieces).reshape(MEMBERS * TOK_MEM, D)
    total = MEMBERS - 1
    weight_fit = (2.0 * fitness_rank.astype(jnp.float32) - total) / total
    scale = (D / MEMBERS) ** 0.5

    def outer(left, right):
        weighted = weight_fit[:, None] * left.astype(jnp.float32)
        return (scale * jnp.dot(weighted.T, right, precision=lax.Precision.HIGHEST, preferred_element_type=jnp.float32)).astype(jnp.bfloat16)

    return mixed, outer(gate_left, gate_right), outer(up_left, up_right)
```

```python
import math

import jax
import jax.numpy as jnp
from jax import lax
from jax.sharding import PartitionSpec as P

noise_scale = 0.5


def silu(value):
    return value / (1.0 + jnp.exp(-value))


def ring_place(index, n):
    return jnp.where(index % 2 == 0, index // 2, n - 1 - index // 2)


def ring_owner(place, n):
    place = place % n
    return jnp.where(place < n // 2, 2 * place, 2 * (n - 1 - place) + 1)


def per_device(
    tokens,
    gate_weight,
    up_weight,
    down_weight,
    gate_left,
    gate_right,
    up_left,
    up_right,
    down_left,
    down_right,
    fitness_rank,
):
    members, width = gate_left.shape
    rows, span = tokens.shape
    per_member = rows // members
    hidden_cols = gate_weight.shape[1]
    n = lax.axis_size("wsh")
    groups = lax.axis_size("grp")
    total_members = members * groups
    hops = n // 2
    half = rows // 2
    wire = jnp.bfloat16 if n <= 8 else jnp.float32

    order = [2 * q for q in range(hops)] + [2 * (n - 1 - q) + 1 for q in range(hops, n)]
    onward = [(order[q], order[(q + 1) % n]) for q in range(n)]
    back = [(b, a) for a, b in onward]
    place = ring_place(lax.axis_index("wsh"), n)

    weight_fit = (2.0 * fitness_rank.astype(jnp.float32) - (total_members - 1)) / (
        total_members - 1
    )
    rights = jnp.concatenate([gate_right, up_right], axis=1)
    fitted = (weight_fit[:, None] * rights).astype(jnp.bfloat16)
    block = width // groups
    grp = lax.axis_index("grp")
    if groups == 4:
        pair = [(g, g ^ 2) for g in range(4)]
        mate = [(g, g ^ 1) for g in range(4)]
        lefts = jnp.stack([gate_left, up_left])
        far = (1 - grp // 2) * 2 * block
        near = (grp // 2) * 2 * block
        away = lax.dynamic_slice_in_dim(lefts, far, 2 * block, 2)
        here = lax.dynamic_slice_in_dim(lefts, near, 2 * block, 2)
        fitted_far = lax.ppermute(fitted, "grp", pair)
        left_far = lax.ppermute(away, "grp", pair)
        fitted_two = jnp.concatenate([fitted, fitted_far], axis=0)
        left_two = jnp.concatenate([here, left_far], axis=1)
        other = (1 - grp % 2) * block
        mine = (grp % 2) * block
        left_out = lax.dynamic_slice_in_dim(left_two, other, block, 2)
        left_own = lax.dynamic_slice_in_dim(left_two, mine, block, 2)
        fitted_in = lax.ppermute(fitted_two, "grp", mate)
        left_in = lax.ppermute(left_out, "grp", mate)
        fitted_all = jnp.concatenate([fitted_two, fitted_in], axis=0)
        left_all = jnp.concatenate([left_own, left_in], axis=1)
        gate_block, up_block = left_all[0], left_all[1]
    else:
        fitted_all = lax.all_gather(fitted, "grp", axis=0, tiled=True)
        gate_all = lax.all_gather(gate_left, "grp", axis=0, tiled=True)
        up_all = lax.all_gather(up_left, "grp", axis=0, tiled=True)
        gate_block = lax.dynamic_slice_in_dim(gate_all, grp * block, block, 1)
        up_block = lax.dynamic_slice_in_dim(up_all, grp * block, block, 1)
    scale = math.sqrt(width / total_members)

    def outer(left, right):
        total = lax.dot_general(
            left, right, (((0,), (0,)), ((), ())), preferred_element_type=jnp.float32
        )
        return (scale * total).astype(jnp.bfloat16)

    gate_step = outer(gate_block, fitted_all[:, :hidden_cols])
    up_step = outer(up_block, fitted_all[:, hidden_cols:])

    left_both = jnp.concatenate([gate_left, up_left], axis=0)

    def grow(total, piece, owner):
        at = owner * span
        gate_w = lax.dynamic_slice_in_dim(gate_weight, at, span, 0)
        up_w = lax.dynamic_slice_in_dim(up_weight, at, span, 0)
        left_w = lax.dynamic_slice_in_dim(left_both, at, span, 1)
        new = (
            jnp.dot(piece, gate_w, preferred_element_type=jnp.float32),
            jnp.dot(piece, up_w, preferred_element_type=jnp.float32),
            lax.dot_general(
                piece, left_w, (((1,), (1,)), ((), ())), preferred_element_type=jnp.float32
            ),
        )
        return new if total is None else tuple(a + b for a, b in zip(total, new))

    from_back, from_front = tokens, tokens
    total = None
    for hop in range(1, hops):
        sent_on, sent_back = from_back, from_front
        from_back = lax.ppermute(sent_on, "wsh", onward)
        from_front = lax.ppermute(sent_back, "wsh", back)
        if hop == 1:
            total = grow(total, tokens, ring_owner(place, n))
        else:
            total = grow(total, sent_on, ring_owner(place - hop + 1, n))
            total = grow(total, sent_back, ring_owner(place + hop - 1, n))
    top = lax.ppermute(from_back[:half], "wsh", onward)
    bottom = lax.ppermute(from_front[half:], "wsh", back)
    total = grow(total, from_back, ring_owner(place - hops + 1, n))
    total = grow(total, from_front, ring_owner(place + hops - 1, n))
    total = grow(total, jnp.concatenate([top, bottom], axis=0), ring_owner(place + hops, n))
    gate_sum, up_sum, scores = total

    own_member = (
        lax.broadcasted_iota(jnp.int32, (rows, members), 0) // per_member
        == lax.broadcasted_iota(jnp.int32, (rows, members), 1)
    )

    def pick(values):
        return jnp.sum(jnp.where(own_member, values, 0.0), axis=1)

    def spread(score, right):
        return (
            score.reshape(members, per_member)[:, :, None] * (noise_scale * right)[:, None, :]
        ).reshape(rows, right.shape[1])

    gate = gate_sum + spread(pick(scores[:, :members]), gate_right)
    up = up_sum + spread(pick(scores[:, members:]), up_right)
    hidden = (silu(gate) * up).astype(jnp.bfloat16)
    down_score = pick(
        lax.dot_general(
            hidden, down_left, (((1,), (1,)), ((), ())), preferred_element_type=jnp.float32
        )
    )

    def share(owner):
        at = owner * span
        down_w = lax.dynamic_slice_in_dim(down_weight, at, span, 1)
        right = lax.dynamic_slice_in_dim(down_right, at, span, 1)
        return jnp.dot(hidden, down_w, preferred_element_type=jnp.float32) + spread(
            down_score, right
        )

    opposite = share(ring_owner(place + hops, n)).astype(wire)
    got_on = lax.ppermute(opposite[:half], "wsh", onward)
    got_back = lax.ppermute(opposite[half:], "wsh", back)
    for hop in range(hops - 1, 0, -1):
        ahead = share(ring_owner(place + hop, n))
        behind = share(ring_owner(place - hop, n))
        if hop == hops - 1:
            ahead = jnp.concatenate([ahead[:half] + got_on.astype(jnp.float32), ahead[half:]], axis=0)
            behind = jnp.concatenate([behind[:half], behind[half:] + got_back.astype(jnp.float32)], axis=0)
        else:
            ahead = ahead + got_on.astype(jnp.float32)
            behind = behind + got_back.astype(jnp.float32)
        got_on = lax.ppermute(ahead.astype(wire), "wsh", onward)
        got_back = lax.ppermute(behind.astype(wire), "wsh", back)
    own = share(ring_owner(place, n))
    mixed = own + got_on.astype(jnp.float32) + got_back.astype(jnp.float32)
    return mixed.astype(jnp.bfloat16), gate_step, up_step


def solution(mesh):
    in_specs = (
        P("grp", "wsh"),
        P(None, "wsh"),
        P(None, "wsh"),
        P("wsh", None),
        P("grp", None),
        P("grp", "wsh"),
        P("grp", None),
        P("grp", "wsh"),
        P("grp", "wsh"),
        P("grp", None),
        P("grp"),
    )
    out_specs = (P("grp", "wsh"), P("grp", "wsh"), P("grp", "wsh"))
    return jax.shard_map(
        per_device, mesh=mesh, in_specs=in_specs, out_specs=out_specs, check_vma=False
    )
```

```python
import math

import jax
import jax.numpy as jnp
from jax import lax
from jax.experimental import pallas as pl
from jax.experimental.pallas import tpu as pltpu
from jax.sharding import PartitionSpec as P

noise_scale = 0.5


def silu(value):
    return value / (1.0 + jnp.exp(-value))


def ring_place(index, n):
    return jnp.where(index % 2 == 0, index // 2, n - 1 - index // 2)


def ring_owner(place, n):
    place = place % n
    return jnp.where(place < n // 2, 2 * place, 2 * (n - 1 - place) + 1)


def plain_device(
    tokens,
    gate_weight,
    up_weight,
    down_weight,
    gate_left,
    gate_right,
    up_left,
    up_right,
    down_left,
    down_right,
    fitness_rank,
):
    members, width = gate_left.shape
    rows, span = tokens.shape
    per_member = rows // members
    hidden_cols = gate_weight.shape[1]
    n = lax.axis_size("wsh")
    groups = lax.axis_size("grp")
    total_members = members * groups
    hops = n // 2
    half = rows // 2
    wire = jnp.bfloat16 if n <= 8 else jnp.float32

    order = [2 * q for q in range(hops)] + [2 * (n - 1 - q) + 1 for q in range(hops, n)]
    onward = [(order[q], order[(q + 1) % n]) for q in range(n)]
    back = [(b, a) for a, b in onward]
    place = ring_place(lax.axis_index("wsh"), n)

    weight_fit = (2.0 * fitness_rank.astype(jnp.float32) - (total_members - 1)) / (
        total_members - 1
    )
    rights = jnp.concatenate([gate_right, up_right], axis=1)
    fitted = (weight_fit[:, None] * rights).astype(jnp.bfloat16)
    block = width // groups
    grp = lax.axis_index("grp")
    if groups == 4:
        pair = [(g, g ^ 2) for g in range(4)]
        mate = [(g, g ^ 1) for g in range(4)]
        lefts = jnp.stack([gate_left, up_left])
        far = (1 - grp // 2) * 2 * block
        near = (grp // 2) * 2 * block
        away = lax.dynamic_slice_in_dim(lefts, far, 2 * block, 2)
        here = lax.dynamic_slice_in_dim(lefts, near, 2 * block, 2)
        fitted_far = lax.ppermute(fitted, "grp", pair)
        left_far = lax.ppermute(away, "grp", pair)
        fitted_two = jnp.concatenate([fitted, fitted_far], axis=0)
        left_two = jnp.concatenate([here, left_far], axis=1)
        other = (1 - grp % 2) * block
        mine = (grp % 2) * block
        left_out = lax.dynamic_slice_in_dim(left_two, other, block, 2)
        left_own = lax.dynamic_slice_in_dim(left_two, mine, block, 2)
        fitted_in = lax.ppermute(fitted_two, "grp", mate)
        left_in = lax.ppermute(left_out, "grp", mate)
        fitted_all = jnp.concatenate([fitted_two, fitted_in], axis=0)
        left_all = jnp.concatenate([left_own, left_in], axis=1)
        gate_block, up_block = left_all[0], left_all[1]
    else:
        fitted_all = lax.all_gather(fitted, "grp", axis=0, tiled=True)
        gate_all = lax.all_gather(gate_left, "grp", axis=0, tiled=True)
        up_all = lax.all_gather(up_left, "grp", axis=0, tiled=True)
        gate_block = lax.dynamic_slice_in_dim(gate_all, grp * block, block, 1)
        up_block = lax.dynamic_slice_in_dim(up_all, grp * block, block, 1)
    scale = math.sqrt(width / total_members)

    def outer(left, right):
        total = lax.dot_general(
            left, right, (((0,), (0,)), ((), ())), preferred_element_type=jnp.float32
        )
        return (scale * total).astype(jnp.bfloat16)

    gate_step = outer(gate_block, fitted_all[:, :hidden_cols])
    up_step = outer(up_block, fitted_all[:, hidden_cols:])

    left_both = jnp.concatenate([gate_left, up_left], axis=0)

    def grow(total, piece, owner):
        at = owner * span
        gate_w = lax.dynamic_slice_in_dim(gate_weight, at, span, 0)
        up_w = lax.dynamic_slice_in_dim(up_weight, at, span, 0)
        left_w = lax.dynamic_slice_in_dim(left_both, at, span, 1)
        new = (
            jnp.dot(piece, gate_w, preferred_element_type=jnp.float32),
            jnp.dot(piece, up_w, preferred_element_type=jnp.float32),
            lax.dot_general(
                piece, left_w, (((1,), (1,)), ((), ())), preferred_element_type=jnp.float32
            ),
        )
        return new if total is None else tuple(a + b for a, b in zip(total, new))

    from_back, from_front = tokens, tokens
    total = None
    for hop in range(1, hops):
        sent_on, sent_back = from_back, from_front
        from_back = lax.ppermute(sent_on, "wsh", onward)
        from_front = lax.ppermute(sent_back, "wsh", back)
        if hop == 1:
            total = grow(total, tokens, ring_owner(place, n))
        else:
            total = grow(total, sent_on, ring_owner(place - hop + 1, n))
            total = grow(total, sent_back, ring_owner(place + hop - 1, n))
    top = lax.ppermute(from_back[:half], "wsh", onward)
    bottom = lax.ppermute(from_front[half:], "wsh", back)
    total = grow(total, from_back, ring_owner(place - hops + 1, n))
    total = grow(total, from_front, ring_owner(place + hops - 1, n))
    total = grow(total, jnp.concatenate([top, bottom], axis=0), ring_owner(place + hops, n))
    gate_sum, up_sum, scores = total

    own_member = (
        lax.broadcasted_iota(jnp.int32, (rows, members), 0) // per_member
        == lax.broadcasted_iota(jnp.int32, (rows, members), 1)
    )

    def pick(values):
        return jnp.sum(jnp.where(own_member, values, 0.0), axis=1)

    def spread(score, right):
        return (
            score.reshape(members, per_member)[:, :, None] * (noise_scale * right)[:, None, :]
        ).reshape(rows, right.shape[1])

    gate = gate_sum + spread(pick(scores[:, :members]), gate_right)
    up = up_sum + spread(pick(scores[:, members:]), up_right)
    hidden = (silu(gate) * up).astype(jnp.bfloat16)
    down_score = pick(
        lax.dot_general(
            hidden, down_left, (((1,), (1,)), ((), ())), preferred_element_type=jnp.float32
        )
    )

    def share(owner):
        at = owner * span
        down_w = lax.dynamic_slice_in_dim(down_weight, at, span, 1)
        right = lax.dynamic_slice_in_dim(down_right, at, span, 1)
        return jnp.dot(hidden, down_w, preferred_element_type=jnp.float32) + spread(
            down_score, right
        )

    opposite = share(ring_owner(place + hops, n)).astype(wire)
    got_on = lax.ppermute(opposite[:half], "wsh", onward)
    got_back = lax.ppermute(opposite[half:], "wsh", back)
    for hop in range(hops - 1, 0, -1):
        ahead = share(ring_owner(place + hop, n))
        behind = share(ring_owner(place - hop, n))
        if hop == hops - 1:
            ahead = jnp.concatenate([ahead[:half] + got_on.astype(jnp.float32), ahead[half:]], axis=0)
            behind = jnp.concatenate([behind[:half], behind[half:] + got_back.astype(jnp.float32)], axis=0)
        else:
            ahead = ahead + got_on.astype(jnp.float32)
            behind = behind + got_back.astype(jnp.float32)
        got_on = lax.ppermute(ahead.astype(wire), "wsh", onward)
        got_back = lax.ppermute(behind.astype(wire), "wsh", back)
    own = share(ring_owner(place, n))
    mixed = own + got_on.astype(jnp.float32) + got_back.astype(jnp.float32)
    return mixed.astype(jnp.bfloat16), gate_step, up_step


MIB = 1 << 20


def dims(lhs, rhs):
    return (((lhs,), (rhs,)), ((), ()))


def message_kernel(at, fit, gate_r, up_r, gate_far, up_far, gate_near, up_near, far, near):
    cols = gate_r.shape[1]
    block = gate_far.shape[1]
    weight = fit[...]
    gate_fit = (weight * gate_r[...]).astype(jnp.bfloat16)
    up_fit = (weight * up_r[...]).astype(jnp.bfloat16)
    for out, gate_l, up_l in ((far, gate_far, up_far), (near, gate_near, up_near)):
        out[:, :cols] = gate_fit
        out[:, cols : 2 * cols] = up_fit
        out[:, 2 * cols : 2 * cols + block] = gate_l[...]
        out[:, 2 * cols + block :] = up_l[...]


def messages(at, fit, gate_right, up_right, gate_left, up_left, slot_far, slot_near):
    members, cols = gate_right.shape
    half_width = gate_left.shape[1] // 2
    shape = jax.ShapeDtypeStruct((members, 2 * cols + 2 * half_width), jnp.bfloat16)
    whole = lambda a: pl.BlockSpec(a.shape, lambda i, at: (0, 0))
    far = pl.BlockSpec((members, half_width), lambda i, at: (0, at[slot_far]))
    near = pl.BlockSpec((members, half_width), lambda i, at: (0, at[slot_near]))
    return pl.pallas_call(
        message_kernel,
        out_shape=(shape, shape),
        grid_spec=pltpu.PrefetchScalarGridSpec(
            num_scalar_prefetch=1,
            grid=(1,),
            in_specs=[whole(fit), whole(gate_right), whole(up_right), far, far, near, near],
            out_specs=[whole(shape), whole(shape)],
        ),
        compiler_params=pltpu.CompilerParams(vmem_limit_bytes=16 * MIB),
        cost_estimate=pl.CostEstimate(flops=10**6, bytes_accessed=2 * 10**6, transcendentals=0),
        name="messages",
    )(at, fit, gate_right, up_right, gate_left, up_left, gate_left, up_left)


def outer_kernel(slot, scale, at, a, b, c, d, gate_out, up_out):
    rows = gate_out.shape[0]
    cols = gate_out.shape[1]
    parts = (a, b, c, d)
    start = pl.multiple_of(2 * cols + at[slot] * rows, 128)
    for out, shift, right_at in ((gate_out, 0, 0), (up_out, 2 * rows, cols)):
        left = jnp.concatenate([p[:, pl.ds(start + shift, rows)] for p in parts], axis=0)
        right = jnp.concatenate([p[:, right_at : right_at + cols] for p in parts], axis=0)
        total = lax.dot_general(left, right, dims(0, 0), preferred_element_type=jnp.float32)
        out[...] = (scale * total).astype(out.dtype)


def outers(at, parts, rows, cols, slot, scale):
    shape = jax.ShapeDtypeStruct((rows, cols), jnp.bfloat16)
    whole = lambda a: pl.BlockSpec(a.shape, lambda i, at: (0, 0))
    return pl.pallas_call(
        lambda *refs: outer_kernel(slot, scale, *refs),
        out_shape=(shape, shape),
        grid_spec=pltpu.PrefetchScalarGridSpec(
            num_scalar_prefetch=1,
            grid=(1,),
            in_specs=[whole(p) for p in parts],
            out_specs=[whole(shape), whole(shape)],
        ),
        compiler_params=pltpu.CompilerParams(vmem_limit_bytes=24 * MIB),
        cost_estimate=pl.CostEstimate(flops=10**9, bytes_accessed=6 * 10**6, transcendentals=0),
        name="outers",
    )(at, *parts)


def grow_kernel(count, fresh, at, *refs):
    pieces = refs[:count]
    gate_w, up_w, gate_l, up_l = refs[count : count + 4]
    old = () if fresh else refs[count + 4 : count + 7]
    gate, up, scores = refs[-3:]
    step = pl.program_id(0)
    for j, piece_ref in enumerate(pieces):

        @pl.when(step == j)
        def _(j=j, piece_ref=piece_ref):
            piece = piece_ref[...]
            left = jnp.concatenate([gate_l[...], up_l[...]], axis=0)
            new_g = jnp.dot(piece, gate_w[...], preferred_element_type=jnp.float32)
            new_u = jnp.dot(piece, up_w[...], preferred_element_type=jnp.float32)
            new_s = lax.dot_general(piece, left, dims(1, 1), preferred_element_type=jnp.float32)
            if j == 0 and fresh:
                gate[...], up[...], scores[...] = new_g, new_u, new_s
            elif j == 0:
                gate[...] = old[0][...] + new_g
                up[...] = old[1][...] + new_u
                scores[...] = old[2][...] + new_s
            else:
                gate[...] += new_g
                up[...] += new_u
                scores[...] += new_s


def grow(at, pieces, slots, gate_weight, up_weight, gate_left, up_left, total):
    rows, span = pieces[0].shape
    cols = gate_weight.shape[1]
    members = gate_left.shape[0]
    count = len(pieces)

    def pick(i, at):
        slot = jnp.int32(slots[0])
        for j in range(1, count):
            slot = jnp.where(i == j, slots[j], slot)
        return at[slot]

    whole = lambda a: pl.BlockSpec(a.shape, lambda i, at: (0, 0))
    weight = pl.BlockSpec((span, cols), lambda i, at: (pick(i, at), 0))
    left = pl.BlockSpec((members, span), lambda i, at: (0, pick(i, at)))
    shapes = (
        jax.ShapeDtypeStruct((rows, cols), jnp.float32),
        jax.ShapeDtypeStruct((rows, cols), jnp.float32),
        jax.ShapeDtypeStruct((rows, 2 * members), jnp.float32),
    )
    old = [] if total is None else list(total)
    return pl.pallas_call(
        lambda *refs: grow_kernel(count, total is None, *refs),
        out_shape=shapes,
        grid_spec=pltpu.PrefetchScalarGridSpec(
            num_scalar_prefetch=1,
            grid=(count,),
            in_specs=[whole(p) for p in pieces] + [weight, weight, left, left] + [whole(o) for o in old],
            out_specs=[whole(s) for s in shapes],
        ),
        compiler_params=pltpu.CompilerParams(vmem_limit_bytes=32 * MIB),
        cost_estimate=pl.CostEstimate(
            flops=count * 2 * rows * span * 2 * cols,
            bytes_accessed=count * span * cols * 4 + 4 * rows * cols * 2 * (1 + len(old) // 3),
            transcendentals=0,
        ),
        name="grow",
    )(at, *pieces, gate_weight, up_weight, gate_left, up_left, *old)


def spread_rows(score, right, per_member):
    members, cols = right.shape
    wide = jnp.broadcast_to(right[:, None, :], (members, per_member, cols))
    return score * wide.reshape(members * per_member, cols)


def hidden_kernel(
    per_member, at, gate_sum, up_sum, scores, top, bottom, gate_w, up_w, gate_l, up_l,
    gate_r, up_r, down_l, down_w, down_r, hidden_out, score_out, share_out,
):
    step = pl.program_id(0)
    steps = pl.num_programs(0)
    rows = gate_sum.shape[0]
    members = gate_l.shape[0]
    local = gate_r.shape[0]
    piece = jnp.where(step < steps // 2, top[...], bottom[...])
    left = jnp.concatenate([gate_l[...], up_l[...]], axis=0)
    score = scores[...] + lax.dot_general(piece, left, dims(1, 1), preferred_element_type=jnp.float32)
    member = lax.broadcasted_iota(jnp.int32, (rows, 2 * members), 0) // per_member + step * local
    column = lax.broadcasted_iota(jnp.int32, (rows, 2 * members), 1)
    gate_score = jnp.sum(jnp.where(column == member, score, 0.0), axis=1, keepdims=True)
    up_score = jnp.sum(jnp.where(column == member + members, score, 0.0), axis=1, keepdims=True)
    gate = gate_sum[...] + jnp.dot(piece, gate_w[...], preferred_element_type=jnp.float32)
    up = up_sum[...] + jnp.dot(piece, up_w[...], preferred_element_type=jnp.float32)
    gate = gate + spread_rows(noise_scale * gate_score, gate_r[...], per_member)
    up = up + spread_rows(noise_scale * up_score, up_r[...], per_member)
    hidden = (silu(gate) * up).astype(jnp.bfloat16)
    hidden_out[...] = hidden
    down = lax.dot_general(hidden, down_l[...], dims(1, 1), preferred_element_type=jnp.float32)
    down = jnp.where(column[:, :members] == member[:, :members], down, 0.0)
    down_score = noise_scale * jnp.sum(down, axis=1, keepdims=True)
    score_out[...] = jnp.broadcast_to(down_score, score_out.shape)
    share = jnp.dot(hidden, down_w[...], preferred_element_type=jnp.float32)
    share_out[...] = (share + spread_rows(down_score, down_r[...], per_member)).astype(share_out.dtype)


def finish(at, total, top, bottom, gate_weight, up_weight, gate_left, up_left, gate_right, up_right,
           down_left, down_weight, down_right, slot, wire):
    rows, cols = total[0].shape
    span = top.shape[1]
    members = gate_left.shape[0]
    per_member = rows // members
    steps = 4
    tall = rows // steps
    local = members // steps
    row = lambda width: pl.BlockSpec((tall, width), lambda i, at: (i, 0))
    whole = lambda a: pl.BlockSpec(a.shape, lambda i, at: (0, 0))
    weight = pl.BlockSpec((span, cols), lambda i, at: (at[slot], 0))
    left = pl.BlockSpec((members, span), lambda i, at: (0, at[slot]))
    return pl.pallas_call(
        lambda *refs: hidden_kernel(per_member, *refs),
        out_shape=(
            jax.ShapeDtypeStruct((rows, cols), jnp.bfloat16),
            jax.ShapeDtypeStruct((rows, 128), jnp.float32),
            jax.ShapeDtypeStruct((rows, span), wire),
        ),
        grid_spec=pltpu.PrefetchScalarGridSpec(
            num_scalar_prefetch=1,
            grid=(steps,),
            in_specs=[
                row(cols), row(cols), row(2 * members),
                pl.BlockSpec((tall, span), lambda i, at: (jnp.minimum(i, steps // 2 - 1), 0)),
                pl.BlockSpec((tall, span), lambda i, at: (jnp.maximum(i - steps // 2, 0), 0)),
                weight, weight, left, left,
                pl.BlockSpec((local, cols), lambda i, at: (i, 0)),
                pl.BlockSpec((local, cols), lambda i, at: (i, 0)),
                whole(down_left),
                pl.BlockSpec((cols, span), lambda i, at: (0, at[slot])),
                pl.BlockSpec((local, span), lambda i, at: (i, at[slot])),
            ],
            out_specs=[row(cols), row(128), row(span)],
        ),
        compiler_params=pltpu.CompilerParams(vmem_limit_bytes=24 * MIB),
        cost_estimate=pl.CostEstimate(
            flops=2 * rows * span * cols * 3, bytes_accessed=6 * 10**6, transcendentals=rows * cols
        ),
        name="finish",
    )(at, *total, top, bottom, gate_weight, up_weight, gate_left, up_left, gate_right, up_right,
      down_left, down_weight, down_right)


def share_kernel(per_member, at, hidden, score, down_w, down_r, out):
    total = jnp.dot(hidden[...], down_w[...], preferred_element_type=jnp.float32)
    out[...] = total + spread_rows(score[...][:, :1], down_r[...], per_member)


def shares(at, hidden, score, down_weight, down_right, slots, span):
    rows, cols = hidden.shape
    members = down_right.shape[0]
    count = len(slots)

    def pick(j, at):
        slot = jnp.int32(slots[0])
        for i in range(1, count):
            slot = jnp.where(j == i, slots[i], slot)
        return at[slot]

    whole = lambda a: pl.BlockSpec(a.shape, lambda j, at: (0, 0))
    return pl.pallas_call(
        lambda *refs: share_kernel(rows // members, *refs),
        out_shape=jax.ShapeDtypeStruct((count, rows, span), jnp.float32),
        grid_spec=pltpu.PrefetchScalarGridSpec(
            num_scalar_prefetch=1,
            grid=(count,),
            in_specs=[
                whole(hidden), whole(score),
                pl.BlockSpec((cols, span), lambda j, at: (0, pick(j, at))),
                pl.BlockSpec((members, span), lambda j, at: (0, pick(j, at))),
            ],
            out_specs=pl.BlockSpec((None, rows, span), lambda j, at: (j, 0, 0)),
        ),
        compiler_params=pltpu.CompilerParams(vmem_limit_bytes=16 * MIB),
        cost_estimate=pl.CostEstimate(
            flops=2 * rows * span * cols * count,
            bytes_accessed=count * span * (2 * cols + 4 * rows),
            transcendentals=0,
        ),
        name="shares",
    )(at, hidden, score, down_weight, down_right)


def per_device(
    tokens,
    gate_weight,
    up_weight,
    down_weight,
    gate_left,
    gate_right,
    up_left,
    up_right,
    down_left,
    down_right,
    fitness_rank,
):
    arguments = (tokens, gate_weight, up_weight, down_weight, gate_left, gate_right, up_left,
                 up_right, down_left, down_right, fitness_rank)
    members, width = gate_left.shape
    rows, span = tokens.shape
    hidden_cols = gate_weight.shape[1]
    n = lax.axis_size("wsh")
    groups = lax.axis_size("grp")
    if n != 8 or groups != 4 or span % 128 or hidden_cols % 128:
        return plain_device(*arguments)
    total_members = members * groups
    hops = n // 2
    half = rows // 2
    wire = jnp.bfloat16

    order = [2 * q for q in range(hops)] + [2 * (n - 1 - q) + 1 for q in range(hops, n)]
    onward = [(order[q], order[(q + 1) % n]) for q in range(n)]
    back = [(b, a) for a, b in onward]
    place = ring_place(lax.axis_index("wsh"), n)
    grp = lax.axis_index("grp")
    at = jnp.concatenate([
        ring_owner(place + jnp.arange(n, dtype=jnp.int32), n),
        jnp.stack([grp // 2, 1 - grp // 2, grp % 2]),
    ]).astype(jnp.int32)
    slot_near, slot_far, slot_core = n, n + 1, n + 2

    pair = [(g, g ^ 2) for g in range(4)]
    mate = [(g, g ^ 1) for g in range(4)]

    one_a = lax.ppermute(tokens, "wsh", onward)
    one_b = lax.ppermute(tokens, "wsh", back)
    weight_fit = (2.0 * fitness_rank.astype(jnp.float32) - (total_members - 1)) / (
        total_members - 1
    )
    far, near = messages(at, weight_fit[:, None], gate_right, up_right, gate_left, up_left, slot_far, slot_near)
    far_in = lax.ppermute(far, "grp", pair)
    near_in = lax.ppermute(near, "grp", mate)
    far_mate = lax.ppermute(far_in, "grp", mate)

    two_a = lax.ppermute(one_a, "wsh", onward)
    two_b = lax.ppermute(one_b, "wsh", back)
    three_a = lax.ppermute(two_a, "wsh", onward)
    three_b = lax.ppermute(two_b, "wsh", back)
    weights = (gate_weight, up_weight, gate_left, up_left)
    total = grow(at, [tokens, one_a, one_b, two_a, two_b], [0, n - 1, 1, n - 2, 2], *weights, None)
    top = lax.ppermute(three_a[:half], "wsh", onward)
    bottom = lax.ppermute(three_b[half:], "wsh", back)
    total = grow(at, [three_a, three_b], [n - 3, 3], *weights, total)
    hidden, score, opposite = finish(
        at, total, top, bottom, *weights, gate_right, up_right, down_left, down_weight, down_right, hops, wire
    )
    got_on = lax.ppermute(opposite[:half], "wsh", onward)
    got_back = lax.ppermute(opposite[half:], "wsh", back)
    rest = shares(at, hidden, score, down_weight, down_right, [3, n - 3, 2, n - 2, 1, n - 1, 0], span)
    wide = lambda a: a.astype(jnp.float32)
    for hop in range(hops - 1, 0, -1):
        ahead = rest[2 * (hops - 1 - hop)]
        behind = rest[2 * (hops - 1 - hop) + 1]
        if hop == hops - 1:
            ahead = jnp.concatenate([ahead[:half] + wide(got_on), ahead[half:]], axis=0)
            behind = jnp.concatenate([behind[:half], behind[half:] + wide(got_back)], axis=0)
        else:
            ahead = ahead + wide(got_on)
            behind = behind + wide(got_back)
        got_on = lax.ppermute(ahead.astype(wire), "wsh", onward)
        got_back = lax.ppermute(behind.astype(wire), "wsh", back)
    mixed = (rest[n - 2] + wide(got_on) + wide(got_back)).astype(jnp.bfloat16)
    scale = math.sqrt(width / total_members)
    gate_step, up_step = outers(at, [near, near_in, far_in, far_mate], width // groups, hidden_cols, slot_core, scale)
    return mixed, gate_step, up_step


def solution(mesh):
    in_specs = (
        P("grp", "wsh"),
        P(None, "wsh"),
        P(None, "wsh"),
        P("wsh", None),
        P("grp", None),
        P("grp", "wsh"),
        P("grp", None),
        P("grp", "wsh"),
        P("grp", "wsh"),
        P("grp", None),
        P("grp"),
    )
    out_specs = (P("grp", "wsh"), P("grp", "wsh"), P("grp", "wsh"))
    return jax.shard_map(
        per_device, mesh=mesh, in_specs=in_specs, out_specs=out_specs, check_vma=False
    )
```

```python
import math

import jax
import jax.numpy as jnp
from jax import lax
from jax.experimental import pallas as pl
from jax.experimental.pallas import tpu as pltpu
from jax.sharding import PartitionSpec as P

noise_scale = 0.5


def silu(value):
    return value / (1.0 + jnp.exp(-value))


def ring_place(index, n):
    return jnp.where(index % 2 == 0, index // 2, n - 1 - index // 2)


def ring_owner(place, n):
    place = place % n
    return jnp.where(place < n // 2, 2 * place, 2 * (n - 1 - place) + 1)


def plain_device(
    tokens,
    gate_weight,
    up_weight,
    down_weight,
    gate_left,
    gate_right,
    up_left,
    up_right,
    down_left,
    down_right,
    fitness_rank,
):
    members, width = gate_left.shape
    rows, span = tokens.shape
    per_member = rows // members
    hidden_cols = gate_weight.shape[1]
    n = lax.axis_size("wsh")
    groups = lax.axis_size("grp")
    total_members = members * groups
    hops = n // 2
    half = rows // 2
    wire = jnp.bfloat16 if n <= 8 else jnp.float32

    order = [2 * q for q in range(hops)] + [2 * (n - 1 - q) + 1 for q in range(hops, n)]
    onward = [(order[q], order[(q + 1) % n]) for q in range(n)]
    back = [(b, a) for a, b in onward]
    place = ring_place(lax.axis_index("wsh"), n)

    weight_fit = (2.0 * fitness_rank.astype(jnp.float32) - (total_members - 1)) / (
        total_members - 1
    )
    rights = jnp.concatenate([gate_right, up_right], axis=1)
    fitted = (weight_fit[:, None] * rights).astype(jnp.bfloat16)
    block = width // groups
    grp = lax.axis_index("grp")
    if groups == 4:
        pair = [(g, g ^ 2) for g in range(4)]
        mate = [(g, g ^ 1) for g in range(4)]
        lefts = jnp.stack([gate_left, up_left])
        far = (1 - grp // 2) * 2 * block
        near = (grp // 2) * 2 * block
        away = lax.dynamic_slice_in_dim(lefts, far, 2 * block, 2)
        here = lax.dynamic_slice_in_dim(lefts, near, 2 * block, 2)
        fitted_far = lax.ppermute(fitted, "grp", pair)
        left_far = lax.ppermute(away, "grp", pair)
        fitted_two = jnp.concatenate([fitted, fitted_far], axis=0)
        left_two = jnp.concatenate([here, left_far], axis=1)
        other = (1 - grp % 2) * block
        mine = (grp % 2) * block
        left_out = lax.dynamic_slice_in_dim(left_two, other, block, 2)
        left_own = lax.dynamic_slice_in_dim(left_two, mine, block, 2)
        fitted_in = lax.ppermute(fitted_two, "grp", mate)
        left_in = lax.ppermute(left_out, "grp", mate)
        fitted_all = jnp.concatenate([fitted_two, fitted_in], axis=0)
        left_all = jnp.concatenate([left_own, left_in], axis=1)
        gate_block, up_block = left_all[0], left_all[1]
    else:
        fitted_all = lax.all_gather(fitted, "grp", axis=0, tiled=True)
        gate_all = lax.all_gather(gate_left, "grp", axis=0, tiled=True)
        up_all = lax.all_gather(up_left, "grp", axis=0, tiled=True)
        gate_block = lax.dynamic_slice_in_dim(gate_all, grp * block, block, 1)
        up_block = lax.dynamic_slice_in_dim(up_all, grp * block, block, 1)
    scale = math.sqrt(width / total_members)

    def outer(left, right):
        total = lax.dot_general(
            left, right, (((0,), (0,)), ((), ())), preferred_element_type=jnp.float32
        )
        return (scale * total).astype(jnp.bfloat16)

    gate_step = outer(gate_block, fitted_all[:, :hidden_cols])
    up_step = outer(up_block, fitted_all[:, hidden_cols:])

    left_both = jnp.concatenate([gate_left, up_left], axis=0)

    def grow(total, piece, owner):
        at = owner * span
        gate_w = lax.dynamic_slice_in_dim(gate_weight, at, span, 0)
        up_w = lax.dynamic_slice_in_dim(up_weight, at, span, 0)
        left_w = lax.dynamic_slice_in_dim(left_both, at, span, 1)
        new = (
            jnp.dot(piece, gate_w, preferred_element_type=jnp.float32),
            jnp.dot(piece, up_w, preferred_element_type=jnp.float32),
            lax.dot_general(
                piece, left_w, (((1,), (1,)), ((), ())), preferred_element_type=jnp.float32
            ),
        )
        return new if total is None else tuple(a + b for a, b in zip(total, new))

    from_back, from_front = tokens, tokens
    total = None
    for hop in range(1, hops):
        sent_on, sent_back = from_back, from_front
        from_back = lax.ppermute(sent_on, "wsh", onward)
        from_front = lax.ppermute(sent_back, "wsh", back)
        if hop == 1:
            total = grow(total, tokens, ring_owner(place, n))
        else:
            total = grow(total, sent_on, ring_owner(place - hop + 1, n))
            total = grow(total, sent_back, ring_owner(place + hop - 1, n))
    top = lax.ppermute(from_back[:half], "wsh", onward)
    bottom = lax.ppermute(from_front[half:], "wsh", back)
    total = grow(total, from_back, ring_owner(place - hops + 1, n))
    total = grow(total, from_front, ring_owner(place + hops - 1, n))
    total = grow(total, jnp.concatenate([top, bottom], axis=0), ring_owner(place + hops, n))
    gate_sum, up_sum, scores = total

    own_member = (
        lax.broadcasted_iota(jnp.int32, (rows, members), 0) // per_member
        == lax.broadcasted_iota(jnp.int32, (rows, members), 1)
    )

    def pick(values):
        return jnp.sum(jnp.where(own_member, values, 0.0), axis=1)

    def spread(score, right):
        return (
            score.reshape(members, per_member)[:, :, None] * (noise_scale * right)[:, None, :]
        ).reshape(rows, right.shape[1])

    gate = gate_sum + spread(pick(scores[:, :members]), gate_right)
    up = up_sum + spread(pick(scores[:, members:]), up_right)
    hidden = (silu(gate) * up).astype(jnp.bfloat16)
    down_score = pick(
        lax.dot_general(
            hidden, down_left, (((1,), (1,)), ((), ())), preferred_element_type=jnp.float32
        )
    )

    def share(owner):
        at = owner * span
        down_w = lax.dynamic_slice_in_dim(down_weight, at, span, 1)
        right = lax.dynamic_slice_in_dim(down_right, at, span, 1)
        return jnp.dot(hidden, down_w, preferred_element_type=jnp.float32) + spread(
            down_score, right
        )

    opposite = share(ring_owner(place + hops, n)).astype(wire)
    got_on = lax.ppermute(opposite[:half], "wsh", onward)
    got_back = lax.ppermute(opposite[half:], "wsh", back)
    for hop in range(hops - 1, 0, -1):
        ahead = share(ring_owner(place + hop, n))
        behind = share(ring_owner(place - hop, n))
        if hop == hops - 1:
            ahead = jnp.concatenate([ahead[:half] + got_on.astype(jnp.float32), ahead[half:]], axis=0)
            behind = jnp.concatenate([behind[:half], behind[half:] + got_back.astype(jnp.float32)], axis=0)
        else:
            ahead = ahead + got_on.astype(jnp.float32)
            behind = behind + got_back.astype(jnp.float32)
        got_on = lax.ppermute(ahead.astype(wire), "wsh", onward)
        got_back = lax.ppermute(behind.astype(wire), "wsh", back)
    own = share(ring_owner(place, n))
    mixed = own + got_on.astype(jnp.float32) + got_back.astype(jnp.float32)
    return mixed.astype(jnp.bfloat16), gate_step, up_step


MIB = 1 << 20
VMEM = pl.BlockSpec(memory_space=pltpu.VMEM)
SMEM = pl.BlockSpec(memory_space=pltpu.SMEM)
ANY = pl.BlockSpec(memory_space=pl.ANY)
HBM = pl.BlockSpec(memory_space=pltpu.HBM)


def dims(lhs, rhs):
    return (((lhs,), (rhs,)), ((), ()))


def call(body, operands, out_shape, micros, name, in_specs=None, out_specs=None, scratch=(), limit=24, aliases=None):
    count = len(out_shape)
    return pl.pallas_call(
        body,
        out_shape=out_shape,
        in_specs=in_specs or [SMEM] + [VMEM] * (len(operands) - 1),
        out_specs=out_specs or (VMEM,) * count,
        scratch_shapes=list(scratch),
        input_output_aliases=aliases or {},
        compiler_params=pltpu.CompilerParams(vmem_limit_bytes=limit * MIB),
        cost_estimate=pl.CostEstimate(flops=int(micros * 10**9), bytes_accessed=10**6, transcendentals=0),
        name=name,
    )(*operands)


def stage_kernel(plan, count, *refs):
    sources, targets, sems = refs[:count], refs[count:-1], refs[-1]
    copies = []
    for i, (target, row) in enumerate(plan):
        height = sources[i].shape[0]
        copies.append(pltpu.make_async_copy(sources[i], targets[target].at[pl.ds(row, height)], sems.at[i]))
    for copy in copies:
        copy.start()
    for copy in copies:
        copy.wait()


def stage(groups, micros, name, earlier=()):
    arrays, plan, shapes = [], [], []
    for target, group in enumerate(groups):
        row = 0
        for array in group:
            arrays.append(pltpu.with_memory_space_constraint(array, pltpu.HBM))
            plan.append((target, row))
            row += array.shape[0]
        shapes.append(pltpu.VMEM((row, group[0].shape[1]), group[0].dtype))
    count = len(arrays)
    staged = call(
        lambda *refs: stage_kernel(plan, count, *refs[:count], *refs[count + len(earlier) :]),
        (*arrays, *earlier),
        tuple(shapes),
        micros,
        name,
        in_specs=[HBM] * count + [ANY] * len(earlier),
        scratch=[pltpu.SemaphoreType.DMA((count,))],
    )
    return [pltpu.with_memory_space_constraint(array, pltpu.VMEM) for array in staged]


def lane_block(ref, index, width, rows=slice(None), base=0):
    return ref[rows, pl.ds(pl.multiple_of(base + index * width, 128), width)]


def message_kernel(slot_far, slot_near, at, fit, rights, lefts, earlier, far, near):
    members = fit.shape[0]
    cols = rights.shape[1]
    block = lefts.shape[1] // 2
    weight = fit[...]
    gate_fit = (weight * rights[:members, :]).astype(jnp.bfloat16)
    up_fit = (weight * rights[members:, :]).astype(jnp.bfloat16)
    for out, slot in ((far, slot_far), (near, slot_near)):
        out[:, :cols] = gate_fit
        out[:, cols : 2 * cols] = up_fit
        out[:, 2 * cols : 2 * cols + block] = lane_block(lefts, at[slot], block, slice(0, members))
        out[:, 2 * cols + block :] = lane_block(lefts, at[slot], block, slice(members, 2 * members))


def messages(at, fit, rights, lefts, earlier, slot_far, slot_near):
    members = fit.shape[0]
    shape = jax.ShapeDtypeStruct((members, 2 * rights.shape[1] + lefts.shape[1]), jnp.bfloat16)
    return call(
        lambda *refs: message_kernel(slot_far, slot_near, *refs),
        (at, fit, rights, lefts, earlier),
        (shape, shape),
        2,
        "messages",
        in_specs=[SMEM] + [VMEM] * 3 + [ANY],
    )


def outer_kernel(slot, scale, at, a, b, c, d, gate_out, up_out):
    rows, cols = gate_out.shape
    parts = (a, b, c, d)
    for out, shift, right_at in ((gate_out, 0, 0), (up_out, 2 * rows, cols)):
        left = jnp.concatenate([lane_block(p, at[slot], rows, base=2 * cols + shift) for p in parts], axis=0)
        right = jnp.concatenate([p[:, right_at : right_at + cols] for p in parts], axis=0)
        total = lax.dot_general(left, right, dims(0, 0), preferred_element_type=jnp.float32)
        out[...] = (scale * total).astype(out.dtype)


def outers(at, parts, rows, cols, slot, scale):
    shape = jax.ShapeDtypeStruct((rows, cols), jnp.bfloat16)
    return call(
        lambda *refs: outer_kernel(slot, scale, *refs), (at, *parts), (shape, shape), 5, "outers"
    )


def row_block(ref, index, height):
    return ref[pl.ds(pl.multiple_of(index * height, height), height), :]


def grow_kernel(slots, first, fresh, tall, at, *refs):
    count = len(slots)
    pieces = refs[:count]
    gate_w, up_w, lefts = refs[count : count + 3]
    old = (None,) * 3 if fresh else refs[count + 3 : count + 6]
    gate, up, scores = refs[-3:]
    rows, span = pieces[0].shape
    members = scores.shape[1] // 2
    owns = [slice(at_row, at_row + members) for at_row in (first, lefts.shape[0] // 2 + first)]
    for start in range(0, rows, tall):
        part = slice(start, start + tall)
        piece = jnp.concatenate([p[part, :] for p in pieces], axis=1)
        for out, was, weight in ((gate, old[0], gate_w), (up, old[1], up_w)):
            rhs = jnp.concatenate([row_block(weight, at[s], span) for s in slots], axis=0)
            new = jnp.dot(piece, rhs, preferred_element_type=jnp.float32)
            out[part, :] = new if fresh else was[part, :] + new
        left = jnp.concatenate(
            [
                jnp.concatenate([lane_block(lefts, at[s], span, own) for s in slots], axis=1)
                for own in owns
            ],
            axis=0,
        )
        new = lax.dot_general(piece, left, dims(1, 1), preferred_element_type=jnp.float32)
        scores[part, :] = new if fresh else old[2][part, :] + new


def grow(at, pieces, slots, weights, total, first, members, micros):
    rows = pieces[0].shape[0]
    cols = weights[0].shape[1]
    count = len(pieces)
    old = () if total is None else tuple(total)
    base = 1 + count + len(weights)
    return call(
        lambda *refs: grow_kernel(slots, first, total is None, min(rows, 256), *refs),
        (at, *pieces, *weights, *old),
        (
            jax.ShapeDtypeStruct((rows, cols), jnp.float32),
            jax.ShapeDtypeStruct((rows, cols), jnp.float32),
            jax.ShapeDtypeStruct((rows, 2 * members), jnp.float32),
        ),
        micros,
        "grow",
        aliases={base + i: i for i in range(len(old))},
    )


def spread_rows(score, right, per_member):
    members, cols = right.shape
    wide = jnp.broadcast_to(right[:, None, :], (members, per_member, cols))
    return score * wide.reshape(members * per_member, cols)


def finish_kernel(
    slot, first, per_member, tall, at, gate_sum, up_sum, scores, top, bottom, gate_w, up_w, lefts,
    rights, down_l, down_w, down_r, hidden_out, score_out, on_out, back_out,
):
    rows = gate_sum.shape[0]
    span = top.shape[1]
    half = rows // 2
    members = rows // per_member
    own = slice(first, first + members)
    gate_rhs, up_rhs = row_block(gate_w, at[slot], span), row_block(up_w, at[slot], span)
    group = lefts.shape[0] // 2
    own_up = slice(group + first, group + first + members)
    left = jnp.concatenate([lane_block(lefts, at[slot], span, own), lane_block(lefts, at[slot], span, own_up)], axis=0)
    down_rhs = lane_block(down_w, at[slot], span)
    down_left = down_l[own, :]
    for start in range(0, rows, tall):
        part = slice(start, start + tall)
        source, shift, out = (top, 0, on_out) if start < half else (bottom, half, back_out)
        inner = slice(start - shift, start - shift + tall)
        mine = slice(first + start // per_member, first + (start + tall) // per_member)
        mine_up = slice(group + mine.start, group + mine.stop)
        piece = source[inner, :]
        score = scores[part, :] + lax.dot_general(piece, left, dims(1, 1), preferred_element_type=jnp.float32)
        member = (lax.broadcasted_iota(jnp.int32, (tall, 2 * members), 0) + start) // per_member
        column = lax.broadcasted_iota(jnp.int32, (tall, 2 * members), 1)
        gate_score = jnp.sum(jnp.where(column == member, score, 0.0), axis=1, keepdims=True)
        up_score = jnp.sum(jnp.where(column == member + members, score, 0.0), axis=1, keepdims=True)
        gate = gate_sum[part, :] + jnp.dot(piece, gate_rhs, preferred_element_type=jnp.float32)
        up = up_sum[part, :] + jnp.dot(piece, up_rhs, preferred_element_type=jnp.float32)
        gate = gate + spread_rows(noise_scale * gate_score, rights[mine, :], per_member)
        up = up + spread_rows(noise_scale * up_score, rights[mine_up, :], per_member)
        hidden = (silu(gate) * up).astype(jnp.bfloat16)
        hidden_out[part, :] = hidden
        down = lax.dot_general(hidden, down_left, dims(1, 1), preferred_element_type=jnp.float32)
        down = jnp.where(column[:, :members] == member[:, :members], down, 0.0)
        down_score = noise_scale * jnp.sum(down, axis=1, keepdims=True)
        score_out[part, :] = jnp.broadcast_to(down_score, (tall, 128))
        share = jnp.dot(hidden, down_rhs, preferred_element_type=jnp.float32)
        share = share + spread_rows(down_score, lane_block(down_r, at[slot], span, mine), per_member)
        out[inner, :] = share.astype(out.dtype)


def finish(at, total, top, bottom, weights, others, slot, first, per_member, wire):
    rows, cols = total[0].shape
    span = top.shape[1]
    return call(
        lambda *refs: finish_kernel(slot, first, per_member, rows // 2, *refs),
        (at, *total, top, bottom, *weights, *others),
        (
            jax.ShapeDtypeStruct((rows, cols), jnp.bfloat16),
            jax.ShapeDtypeStruct((rows, 128), jnp.float32),
            jax.ShapeDtypeStruct((rows // 2, span), wire),
            jax.ShapeDtypeStruct((rows // 2, span), wire),
        ),
        4,
        "finish",
    )


def share_kernel(slots, first, per_member, at, hidden, score, down_w, down_r, *outs):
    rows = hidden.shape[0]
    own = slice(first, first + rows // per_member)
    for slot, out in zip(slots, outs):
        span = out.shape[1]
        total = jnp.dot(hidden[...], lane_block(down_w, at[slot], span), preferred_element_type=jnp.float32)
        out[...] = total + spread_rows(score[:, :1], lane_block(down_r, at[slot], span, own), per_member)


def shares(at, hidden, score, down_weight, down_right, slots, span, first, per_member, micros, passing=()):
    count = len(slots)
    shape = jax.ShapeDtypeStruct((hidden.shape[0], span), jnp.float32)
    return call(
        lambda *refs: share_kernel(slots, first, per_member, *refs[:5], *refs[5 + len(passing) :][:count]),
        (at, hidden, score, down_weight, down_right, *passing),
        (shape,) * count + tuple(jax.ShapeDtypeStruct(p.shape, p.dtype) for p in passing),
        micros,
        "shares",
        in_specs=[SMEM] + [VMEM] * 4 + [ANY] * len(passing),
        out_specs=(VMEM,) * count + (ANY,) * len(passing),
        aliases={5 + i: count + i for i in range(len(passing))},
    )


CHUNKS = 1


def per_device(
    tokens,
    gate_weight,
    up_weight,
    down_weight,
    gate_left,
    gate_right,
    up_left,
    up_right,
    down_left,
    down_right,
    fitness_rank,
):
    arguments = (tokens, gate_weight, up_weight, down_weight, gate_left, gate_right, up_left,
                 up_right, down_left, down_right, fitness_rank)
    members, width = gate_left.shape
    all_rows, span = tokens.shape
    hidden_cols = gate_weight.shape[1]
    n = lax.axis_size("wsh")
    groups = lax.axis_size("grp")
    if n != 8 or groups != 4 or span % 128 or hidden_cols % 128:
        return plain_device(*arguments)
    total_members = members * groups
    per_member = all_rows // members
    hops = n // 2
    rows = all_rows // CHUNKS
    half = rows // 2
    wire = jnp.bfloat16

    order = [2 * q for q in range(hops)] + [2 * (n - 1 - q) + 1 for q in range(hops, n)]
    onward = [(order[q], order[(q + 1) % n]) for q in range(n)]
    back = [(b, a) for a, b in onward]
    place = ring_place(lax.axis_index("wsh"), n)
    grp = lax.axis_index("grp")
    at = jnp.concatenate([
        ring_owner(place + jnp.arange(n, dtype=jnp.int32), n),
        jnp.stack([grp // 2, 1 - grp // 2, grp % 2]),
    ]).astype(jnp.int32)
    slot_near, slot_far, slot_core = n, n + 1, n + 2

    pair = [(g, g ^ 2) for g in range(4)]
    mate = [(g, g ^ 1) for g in range(4)]
    on = lambda a: lax.ppermute(a, "wsh", onward)
    back_to = lambda a: lax.ppermute(a, "wsh", back)

    weight_fit = (2.0 * fitness_rank.astype(jnp.float32) - (total_members - 1)) / (
        total_members - 1
    )
    lefts, gate_w, up_w = stage([(gate_left, up_left), (gate_weight,), (up_weight,)], 4, "stage_one")
    weights = (gate_w, up_w, lefts)

    wide = lambda a: a.astype(jnp.float32)

    def gather(piece, first):
        count = rows // per_member
        micros = 5 / CHUNKS
        a = b = piece
        total, early = None, []
        pieces, slots = [piece], [0]
        for hop in range(1, hops):
            a, b = on(a), back_to(b)
            if hop > 1:
                total = grow(at, pieces, slots, weights, total, first, count, micros)
                pieces, slots = [], []
                early.append(total[2])
            pieces, slots = pieces + [a, b], slots + [n - hop, hop]
        top, bottom = on(a[:half]), back_to(b[half:])
        total = grow(at, pieces, slots, weights, total, first, count, micros)
        return total, top, bottom, early

    def scatter(hidden, score, opposite_on, opposite_back, first, passed):
        got_on, got_back = on(opposite_on), back_to(opposite_back)
        micros = 4 / CHUNKS
        rest = []
        for hop in range(hops - 1, 0, -1):
            slots = [hop, n - hop] if hop > 1 else [hop, n - hop, 0]
            passing = () if hop > 1 else (passed,)
            rest.append(shares(at, hidden, score, down_w, down_r, slots, span, first, per_member, micros, passing))
            ahead, behind = rest[-1][:2]
            if hop == hops - 1:
                ahead = jnp.concatenate([ahead[:half] + wide(got_on), ahead[half:]], axis=0)
                behind = jnp.concatenate([behind[:half], behind[half:] + wide(got_back)], axis=0)
            else:
                ahead = ahead + wide(got_on)
                behind = behind + wide(got_back)
            got_on, got_back = on(ahead.astype(wire)), back_to(behind.astype(wire))
        return (rest[-1][2] + wide(got_on) + wide(got_back)).astype(jnp.bfloat16), rest[-1][3]

    outs = []
    for chunk in range(CHUNKS):
        first = chunk * members // CHUNKS
        total, top, bottom, early = gather(tokens[chunk * rows : (chunk + 1) * rows], first)
        if chunk == 0:
            rights, down_l, down_r, down_w = stage(
                [(gate_right, up_right), (down_left,), (down_right,), (down_weight,)], 2, "stage_two", early[:1]
            )
            others = (rights, down_l, down_w, down_r)
            far, near = messages(at, weight_fit[:, None], rights, lefts, early[1], slot_far, slot_near)
            far_in = lax.ppermute(far, "grp", pair)
            near_in = lax.ppermute(near, "grp", mate)
        made = finish(at, total, top, bottom, weights, others, hops, first, per_member, wire)
        outs.append((made, first))
    mixed = []
    for made, first in outs:
        done, far_in = scatter(*made, first, far_in)
        mixed.append(done)
    far_mate = lax.ppermute(far_in, "grp", mate)
    mixed = mixed[0] if CHUNKS == 1 else jnp.concatenate(mixed, axis=0)
    scale = math.sqrt(width / total_members)
    gate_step, up_step = outers(at, [near, near_in, far_in, far_mate], width // groups, hidden_cols, slot_core, scale)
    return mixed, gate_step, up_step


def solution(mesh):
    in_specs = (
        P("grp", "wsh"),
        P(None, "wsh"),
        P(None, "wsh"),
        P("wsh", None),
        P("grp", None),
        P("grp", "wsh"),
        P("grp", None),
        P("grp", "wsh"),
        P("grp", "wsh"),
        P("grp", None),
        P("grp"),
    )
    out_specs = (P("grp", "wsh"), P("grp", "wsh"), P("grp", "wsh"))
    return jax.shard_map(
        per_device, mesh=mesh, in_specs=in_specs, out_specs=out_specs, check_vma=False
    )
```

```python
import math

import jax
import jax.numpy as jnp
from jax import lax
from jax.experimental import pallas as pl
from jax.experimental.pallas import tpu as pltpu
from jax.sharding import PartitionSpec as P

noise_scale = 0.5


def silu(value):
    return value / (1.0 + jnp.exp(-value))


def ring_place(index, n):
    return jnp.where(index % 2 == 0, index // 2, n - 1 - index // 2)


def ring_owner(place, n):
    place = place % n
    return jnp.where(place < n // 2, 2 * place, 2 * (n - 1 - place) + 1)


def plain_device(
    tokens,
    gate_weight,
    up_weight,
    down_weight,
    gate_left,
    gate_right,
    up_left,
    up_right,
    down_left,
    down_right,
    fitness_rank,
):
    members, width = gate_left.shape
    rows, span = tokens.shape
    per_member = rows // members
    hidden_cols = gate_weight.shape[1]
    n = lax.axis_size("wsh")
    groups = lax.axis_size("grp")
    total_members = members * groups
    hops = n // 2
    half = rows // 2
    wire = jnp.bfloat16 if n <= 8 else jnp.float32

    order = [2 * q for q in range(hops)] + [2 * (n - 1 - q) + 1 for q in range(hops, n)]
    onward = [(order[q], order[(q + 1) % n]) for q in range(n)]
    back = [(b, a) for a, b in onward]
    place = ring_place(lax.axis_index("wsh"), n)

    weight_fit = (2.0 * fitness_rank.astype(jnp.float32) - (total_members - 1)) / (
        total_members - 1
    )
    rights = jnp.concatenate([gate_right, up_right], axis=1)
    fitted = (weight_fit[:, None] * rights).astype(jnp.bfloat16)
    block = width // groups
    grp = lax.axis_index("grp")
    if groups == 4:
        pair = [(g, g ^ 2) for g in range(4)]
        mate = [(g, g ^ 1) for g in range(4)]
        lefts = jnp.stack([gate_left, up_left])
        far = (1 - grp // 2) * 2 * block
        near = (grp // 2) * 2 * block
        away = lax.dynamic_slice_in_dim(lefts, far, 2 * block, 2)
        here = lax.dynamic_slice_in_dim(lefts, near, 2 * block, 2)
        fitted_far = lax.ppermute(fitted, "grp", pair)
        left_far = lax.ppermute(away, "grp", pair)
        fitted_two = jnp.concatenate([fitted, fitted_far], axis=0)
        left_two = jnp.concatenate([here, left_far], axis=1)
        other = (1 - grp % 2) * block
        mine = (grp % 2) * block
        left_out = lax.dynamic_slice_in_dim(left_two, other, block, 2)
        left_own = lax.dynamic_slice_in_dim(left_two, mine, block, 2)
        fitted_in = lax.ppermute(fitted_two, "grp", mate)
        left_in = lax.ppermute(left_out, "grp", mate)
        fitted_all = jnp.concatenate([fitted_two, fitted_in], axis=0)
        left_all = jnp.concatenate([left_own, left_in], axis=1)
        gate_block, up_block = left_all[0], left_all[1]
    else:
        fitted_all = lax.all_gather(fitted, "grp", axis=0, tiled=True)
        gate_all = lax.all_gather(gate_left, "grp", axis=0, tiled=True)
        up_all = lax.all_gather(up_left, "grp", axis=0, tiled=True)
        gate_block = lax.dynamic_slice_in_dim(gate_all, grp * block, block, 1)
        up_block = lax.dynamic_slice_in_dim(up_all, grp * block, block, 1)
    scale = math.sqrt(width / total_members)

    def outer(left, right):
        total = lax.dot_general(
            left, right, (((0,), (0,)), ((), ())), preferred_element_type=jnp.float32
        )
        return (scale * total).astype(jnp.bfloat16)

    gate_step = outer(gate_block, fitted_all[:, :hidden_cols])
    up_step = outer(up_block, fitted_all[:, hidden_cols:])

    left_both = jnp.concatenate([gate_left, up_left], axis=0)

    def grow(total, piece, owner):
        at = owner * span
        gate_w = lax.dynamic_slice_in_dim(gate_weight, at, span, 0)
        up_w = lax.dynamic_slice_in_dim(up_weight, at, span, 0)
        left_w = lax.dynamic_slice_in_dim(left_both, at, span, 1)
        new = (
            jnp.dot(piece, gate_w, preferred_element_type=jnp.float32),
            jnp.dot(piece, up_w, preferred_element_type=jnp.float32),
            lax.dot_general(
                piece, left_w, (((1,), (1,)), ((), ())), preferred_element_type=jnp.float32
            ),
        )
        return new if total is None else tuple(a + b for a, b in zip(total, new))

    from_back, from_front = tokens, tokens
    total = None
    for hop in range(1, hops):
        sent_on, sent_back = from_back, from_front
        from_back = lax.ppermute(sent_on, "wsh", onward)
        from_front = lax.ppermute(sent_back, "wsh", back)
        if hop == 1:
            total = grow(total, tokens, ring_owner(place, n))
        else:
            total = grow(total, sent_on, ring_owner(place - hop + 1, n))
            total = grow(total, sent_back, ring_owner(place + hop - 1, n))
    top = lax.ppermute(from_back[:half], "wsh", onward)
    bottom = lax.ppermute(from_front[half:], "wsh", back)
    total = grow(total, from_back, ring_owner(place - hops + 1, n))
    total = grow(total, from_front, ring_owner(place + hops - 1, n))
    total = grow(total, jnp.concatenate([top, bottom], axis=0), ring_owner(place + hops, n))
    gate_sum, up_sum, scores = total

    own_member = (
        lax.broadcasted_iota(jnp.int32, (rows, members), 0) // per_member
        == lax.broadcasted_iota(jnp.int32, (rows, members), 1)
    )

    def pick(values):
        return jnp.sum(jnp.where(own_member, values, 0.0), axis=1)

    def spread(score, right):
        return (
            score.reshape(members, per_member)[:, :, None] * (noise_scale * right)[:, None, :]
        ).reshape(rows, right.shape[1])

    gate = gate_sum + spread(pick(scores[:, :members]), gate_right)
    up = up_sum + spread(pick(scores[:, members:]), up_right)
    hidden = (silu(gate) * up).astype(jnp.bfloat16)
    down_score = pick(
        lax.dot_general(
            hidden, down_left, (((1,), (1,)), ((), ())), preferred_element_type=jnp.float32
        )
    )

    def share(owner):
        at = owner * span
        down_w = lax.dynamic_slice_in_dim(down_weight, at, span, 1)
        right = lax.dynamic_slice_in_dim(down_right, at, span, 1)
        return jnp.dot(hidden, down_w, preferred_element_type=jnp.float32) + spread(
            down_score, right
        )

    opposite = share(ring_owner(place + hops, n)).astype(wire)
    got_on = lax.ppermute(opposite[:half], "wsh", onward)
    got_back = lax.ppermute(opposite[half:], "wsh", back)
    for hop in range(hops - 1, 0, -1):
        ahead = share(ring_owner(place + hop, n))
        behind = share(ring_owner(place - hop, n))
        if hop == hops - 1:
            ahead = jnp.concatenate([ahead[:half] + got_on.astype(jnp.float32), ahead[half:]], axis=0)
            behind = jnp.concatenate([behind[:half], behind[half:] + got_back.astype(jnp.float32)], axis=0)
        else:
            ahead = ahead + got_on.astype(jnp.float32)
            behind = behind + got_back.astype(jnp.float32)
        got_on = lax.ppermute(ahead.astype(wire), "wsh", onward)
        got_back = lax.ppermute(behind.astype(wire), "wsh", back)
    own = share(ring_owner(place, n))
    mixed = own + got_on.astype(jnp.float32) + got_back.astype(jnp.float32)
    return mixed.astype(jnp.bfloat16), gate_step, up_step


MIB = 1 << 20
VMEM = pl.BlockSpec(memory_space=pltpu.VMEM)
SMEM = pl.BlockSpec(memory_space=pltpu.SMEM)
ANY = pl.BlockSpec(memory_space=pl.ANY)
HBM = pl.BlockSpec(memory_space=pltpu.HBM)


def dims(lhs, rhs):
    return (((lhs,), (rhs,)), ((), ()))


def call(body, operands, out_shape, micros, name, in_specs=None, out_specs=None, scratch=(), limit=24, aliases=None):
    count = len(out_shape)
    return pl.pallas_call(
        body,
        out_shape=out_shape,
        in_specs=in_specs or [SMEM] + [VMEM] * (len(operands) - 1),
        out_specs=out_specs or (VMEM,) * count,
        scratch_shapes=list(scratch),
        input_output_aliases=aliases or {},
        compiler_params=pltpu.CompilerParams(vmem_limit_bytes=limit * MIB),
        cost_estimate=pl.CostEstimate(flops=int(micros * 10**9), bytes_accessed=10**6, transcendentals=0),
        name=name,
    )(*operands)


def stage_kernel(plan, count, *refs):
    sources, targets, sems = refs[:count], refs[count:-1], refs[-1]
    copies = []
    for i, (target, row) in enumerate(plan):
        height = sources[i].shape[0]
        copies.append(pltpu.make_async_copy(sources[i], targets[target].at[pl.ds(row, height)], sems.at[i]))
    for copy in copies:
        copy.start()
    for copy in copies:
        copy.wait()


def stage(groups, micros, name, earlier=()):
    arrays, plan, shapes = [], [], []
    for target, group in enumerate(groups):
        row = 0
        for array in group:
            arrays.append(pltpu.with_memory_space_constraint(array, pltpu.HBM))
            plan.append((target, row))
            row += array.shape[0]
        shapes.append(pltpu.VMEM((row, group[0].shape[1]), group[0].dtype))
    count = len(arrays)
    staged = call(
        lambda *refs: stage_kernel(plan, count, *refs[:count], *refs[count + len(earlier) :]),
        (*arrays, *earlier),
        tuple(shapes),
        micros,
        name,
        in_specs=[HBM] * count + [ANY] * len(earlier),
        scratch=[pltpu.SemaphoreType.DMA((count,))],
    )
    return [pltpu.with_memory_space_constraint(array, pltpu.VMEM) for array in staged]


def lane_block(ref, index, width, rows=slice(None), base=0):
    return ref[rows, pl.ds(pl.multiple_of(base + index * width, 128), width)]


def message_kernel(slot_far, slot_near, at, fit, rights, lefts, earlier, far, near):
    members = fit.shape[0]
    cols = rights.shape[1]
    block = lefts.shape[1] // 2
    weight = fit[...]
    gate_fit = (weight * rights[:members, :]).astype(jnp.bfloat16)
    up_fit = (weight * rights[members:, :]).astype(jnp.bfloat16)
    for out, slot in ((far, slot_far), (near, slot_near)):
        out[:, :cols] = gate_fit
        out[:, cols : 2 * cols] = up_fit
        out[:, 2 * cols : 2 * cols + block] = lane_block(lefts, at[slot], block, slice(0, members))
        out[:, 2 * cols + block :] = lane_block(lefts, at[slot], block, slice(members, 2 * members))


def messages(at, fit, rights, lefts, earlier, slot_far, slot_near):
    members = fit.shape[0]
    shape = jax.ShapeDtypeStruct((members, 2 * rights.shape[1] + lefts.shape[1]), jnp.bfloat16)
    return call(
        lambda *refs: message_kernel(slot_far, slot_near, *refs),
        (at, fit, rights, lefts, earlier),
        (shape, shape),
        2,
        "messages",
        in_specs=[SMEM] + [VMEM] * 3 + [ANY],
    )


def outer_kernel(slot, scale, at, a, b, c, d, gate_out, up_out):
    rows, cols = gate_out.shape
    parts = (a, b, c, d)
    for out, shift, right_at in ((gate_out, 0, 0), (up_out, 2 * rows, cols)):
        left = jnp.concatenate([lane_block(p, at[slot], rows, base=2 * cols + shift) for p in parts], axis=0)
        right = jnp.concatenate([p[:, right_at : right_at + cols] for p in parts], axis=0)
        total = lax.dot_general(left, right, dims(0, 0), preferred_element_type=jnp.float32)
        out[...] = (scale * total).astype(out.dtype)


def outers(at, parts, rows, cols, slot, scale):
    shape = jax.ShapeDtypeStruct((rows, cols), jnp.bfloat16)
    return call(
        lambda *refs: outer_kernel(slot, scale, *refs), (at, *parts), (shape, shape), 5, "outers"
    )


def row_block(ref, index, height):
    return ref[pl.ds(pl.multiple_of(index * height, height), height), :]


def grow_kernel(slots, first, fresh, tall, at, *refs):
    count = len(slots)
    pieces = refs[:count]
    gate_w, up_w, lefts = refs[count : count + 3]
    old = (None,) * 3 if fresh else refs[count + 3 : count + 6]
    gate, up, scores = refs[-3:]
    rows, span = pieces[0].shape
    members = scores.shape[1] // 2
    owns = [slice(at_row, at_row + members) for at_row in (first, lefts.shape[0] // 2 + first)]
    for start in range(0, rows, tall):
        part = slice(start, start + tall)
        piece = jnp.concatenate([p[part, :] for p in pieces], axis=1)
        for out, was, weight in ((gate, old[0], gate_w), (up, old[1], up_w)):
            rhs = jnp.concatenate([row_block(weight, at[s], span) for s in slots], axis=0)
            new = jnp.dot(piece, rhs, preferred_element_type=jnp.float32)
            out[part, :] = new if fresh else was[part, :] + new
        left = jnp.concatenate(
            [
                jnp.concatenate([lane_block(lefts, at[s], span, own) for s in slots], axis=1)
                for own in owns
            ],
            axis=0,
        )
        new = lax.dot_general(piece, left, dims(1, 1), preferred_element_type=jnp.float32)
        scores[part, :] = new if fresh else old[2][part, :] + new


def grow(at, pieces, slots, weights, total, first, members, micros):
    rows = pieces[0].shape[0]
    cols = weights[0].shape[1]
    count = len(pieces)
    old = () if total is None else tuple(total)
    base = 1 + count + len(weights)
    return call(
        lambda *refs: grow_kernel(slots, first, total is None, min(rows, 256), *refs),
        (at, *pieces, *weights, *old),
        (
            jax.ShapeDtypeStruct((rows, cols), jnp.float32),
            jax.ShapeDtypeStruct((rows, cols), jnp.float32),
            jax.ShapeDtypeStruct((rows, 2 * members), jnp.float32),
        ),
        micros,
        "grow",
        aliases={base + i: i for i in range(len(old))},
    )


def spread_rows(score, right, per_member):
    members, cols = right.shape
    wide = jnp.broadcast_to(right[:, None, :], (members, per_member, cols))
    return score * wide.reshape(members * per_member, cols)


def finish_kernel(
    slot, first, per_member, tall, at, gate_sum, up_sum, scores, top, bottom, gate_w, up_w, lefts,
    rights, down_l, down_w, down_r, hidden_out, score_out, on_out, back_out,
):
    rows = gate_sum.shape[0]
    span = top.shape[1]
    half = rows // 2
    members = rows // per_member
    own = slice(first, first + members)
    gate_rhs, up_rhs = row_block(gate_w, at[slot], span), row_block(up_w, at[slot], span)
    group = lefts.shape[0] // 2
    own_up = slice(group + first, group + first + members)
    left = jnp.concatenate([lane_block(lefts, at[slot], span, own), lane_block(lefts, at[slot], span, own_up)], axis=0)
    down_rhs = lane_block(down_w, at[slot], span)
    down_left = down_l[own, :]
    for start in range(0, rows, tall):
        part = slice(start, start + tall)
        source, shift, out = (top, 0, on_out) if start < half else (bottom, half, back_out)
        inner = slice(start - shift, start - shift + tall)
        mine = slice(first + start // per_member, first + (start + tall) // per_member)
        mine_up = slice(group + mine.start, group + mine.stop)
        piece = source[inner, :]
        score = scores[part, :] + lax.dot_general(piece, left, dims(1, 1), preferred_element_type=jnp.float32)
        member = (lax.broadcasted_iota(jnp.int32, (tall, 2 * members), 0) + start) // per_member
        column = lax.broadcasted_iota(jnp.int32, (tall, 2 * members), 1)
        gate_score = jnp.sum(jnp.where(column == member, score, 0.0), axis=1, keepdims=True)
        up_score = jnp.sum(jnp.where(column == member + members, score, 0.0), axis=1, keepdims=True)
        gate = gate_sum[part, :] + jnp.dot(piece, gate_rhs, preferred_element_type=jnp.float32)
        up = up_sum[part, :] + jnp.dot(piece, up_rhs, preferred_element_type=jnp.float32)
        gate = gate + spread_rows(noise_scale * gate_score, rights[mine, :], per_member)
        up = up + spread_rows(noise_scale * up_score, rights[mine_up, :], per_member)
        hidden = (silu(gate) * up).astype(jnp.bfloat16)
        hidden_out[part, :] = hidden
        down = lax.dot_general(hidden, down_left, dims(1, 1), preferred_element_type=jnp.float32)
        down = jnp.where(column[:, :members] == member[:, :members], down, 0.0)
        down_score = noise_scale * jnp.sum(down, axis=1, keepdims=True)
        score_out[part, :] = jnp.broadcast_to(down_score, (tall, 128))
        share = jnp.dot(hidden, down_rhs, preferred_element_type=jnp.float32)
        share = share + spread_rows(down_score, lane_block(down_r, at[slot], span, mine), per_member)
        out[inner, :] = share.astype(out.dtype)


def finish(at, total, top, bottom, weights, others, slot, first, per_member, wire):
    rows, cols = total[0].shape
    span = top.shape[1]
    return call(
        lambda *refs: finish_kernel(slot, first, per_member, rows // 2, *refs),
        (at, *total, top, bottom, *weights, *others),
        (
            jax.ShapeDtypeStruct((rows, cols), jnp.bfloat16),
            jax.ShapeDtypeStruct((rows, 128), jnp.float32),
            jax.ShapeDtypeStruct((rows // 2, span), wire),
            jax.ShapeDtypeStruct((rows // 2, span), wire),
        ),
        4,
        "finish",
    )


def share_kernel(slots, first, per_member, at, hidden, score, down_w, down_r, *outs):
    rows = hidden.shape[0]
    own = slice(first, first + rows // per_member)
    for slot, out in zip(slots, outs):
        span = out.shape[1]
        total = jnp.dot(hidden[...], lane_block(down_w, at[slot], span), preferred_element_type=jnp.float32)
        out[...] = total + spread_rows(score[:, :1], lane_block(down_r, at[slot], span, own), per_member)


def shares(at, hidden, score, down_weight, down_right, slots, span, first, per_member, micros, passing=()):
    count = len(slots)
    shape = jax.ShapeDtypeStruct((hidden.shape[0], span), jnp.float32)
    return call(
        lambda *refs: share_kernel(slots, first, per_member, *refs[:5], *refs[5 + len(passing) :][:count]),
        (at, hidden, score, down_weight, down_right, *passing),
        (shape,) * count + tuple(jax.ShapeDtypeStruct(p.shape, p.dtype) for p in passing),
        micros,
        "shares",
        in_specs=[SMEM] + [VMEM] * 4 + [ANY] * len(passing),
        out_specs=(VMEM,) * count + (ANY,) * len(passing),
        aliases={5 + i: count + i for i in range(len(passing))},
    )


CHUNKS = 1


def per_device(
    tokens,
    gate_weight,
    up_weight,
    down_weight,
    gate_left,
    gate_right,
    up_left,
    up_right,
    down_left,
    down_right,
    fitness_rank,
):
    arguments = (tokens, gate_weight, up_weight, down_weight, gate_left, gate_right, up_left,
                 up_right, down_left, down_right, fitness_rank)
    members, width = gate_left.shape
    all_rows, span = tokens.shape
    hidden_cols = gate_weight.shape[1]
    n = lax.axis_size("wsh")
    groups = lax.axis_size("grp")
    if n != 8 or groups != 4 or span % 128 or hidden_cols % 128:
        return plain_device(*arguments)
    total_members = members * groups
    per_member = all_rows // members
    hops = n // 2
    rows = all_rows // CHUNKS
    half = rows // 2
    wire = jnp.bfloat16

    order = [2 * q for q in range(hops)] + [2 * (n - 1 - q) + 1 for q in range(hops, n)]
    onward = [(order[q], order[(q + 1) % n]) for q in range(n)]
    back = [(b, a) for a, b in onward]
    place = ring_place(lax.axis_index("wsh"), n)
    grp = lax.axis_index("grp")
    at = jnp.concatenate([
        ring_owner(place + jnp.arange(n, dtype=jnp.int32), n),
        jnp.stack([grp // 2, 1 - grp // 2, grp % 2]),
    ]).astype(jnp.int32)
    slot_near, slot_far, slot_core = n, n + 1, n + 2

    pair = [(g, g ^ 2) for g in range(4)]
    mate = [(g, g ^ 1) for g in range(4)]
    on = lambda a: lax.ppermute(a, "wsh", onward)
    back_to = lambda a: lax.ppermute(a, "wsh", back)

    weight_fit = (2.0 * fitness_rank.astype(jnp.float32) - (total_members - 1)) / (
        total_members - 1
    )
    lefts, gate_w, up_w = stage([(gate_left, up_left), (gate_weight,), (up_weight,)], 4, "stage_one")
    weights = (gate_w, up_w, lefts)

    wide = lambda a: a.astype(jnp.float32)

    def gather(piece, first):
        count = rows // per_member
        micros = 5 / CHUNKS
        a = b = piece
        total, early = None, []
        pieces, slots = [piece], [0]
        for hop in range(1, hops):
            a, b = on(a), back_to(b)
            if hop > 1:
                total = grow(at, pieces, slots, weights, total, first, count, micros)
                pieces, slots = [], []
                early.append(total[2])
            pieces, slots = pieces + [a, b], slots + [n - hop, hop]
        top, bottom = on(a[:half]), back_to(b[half:])
        total = grow(at, pieces, slots, weights, total, first, count, micros)
        return total, top, bottom, early

    def scatter(hidden, score, opposite_on, opposite_back, first, passed):
        got_on, got_back = on(opposite_on), back_to(opposite_back)
        micros = 4 / CHUNKS
        rest = []
        for hop in range(hops - 1, 0, -1):
            slots = [hop, n - hop] if hop > 1 else [hop, n - hop, 0]
            passing = (passed,) if hop == 3 else ()
            rest.append(shares(at, hidden, score, down_w, down_r, slots, span, first, per_member, micros, passing))
            ahead, behind = rest[-1][:2]
            if hop == hops - 1:
                ahead = jnp.concatenate([ahead[:half] + wide(got_on), ahead[half:]], axis=0)
                behind = jnp.concatenate([behind[:half], behind[half:] + wide(got_back)], axis=0)
            else:
                ahead = ahead + wide(got_on)
                behind = behind + wide(got_back)
            got_on, got_back = on(ahead.astype(wire)), back_to(behind.astype(wire))
        return (rest[-1][2] + wide(got_on) + wide(got_back)).astype(jnp.bfloat16), rest[-3][2]

    outs = []
    for chunk in range(CHUNKS):
        first = chunk * members // CHUNKS
        total, top, bottom, early = gather(tokens[chunk * rows : (chunk + 1) * rows], first)
        if chunk == 0:
            rights, down_l, down_r, down_w = stage(
                [(gate_right, up_right), (down_left,), (down_right,), (down_weight,)], 2, "stage_two", early[:1]
            )
            others = (rights, down_l, down_w, down_r)
            far, near = messages(at, weight_fit[:, None], rights, lefts, early[1], slot_far, slot_near)
            far_in = lax.ppermute(far, "grp", pair)
            near_in = lax.ppermute(near, "grp", mate)
        made = finish(at, total, top, bottom, weights, others, hops, first, per_member, wire)
        outs.append((made, first))
    mixed = []
    for made, first in outs:
        done, far_in = scatter(*made, first, far_in)
        mixed.append(done)
    far_mate = lax.ppermute(far_in, "grp", mate)
    mixed = mixed[0] if CHUNKS == 1 else jnp.concatenate(mixed, axis=0)
    scale = math.sqrt(width / total_members)
    gate_step, up_step = outers(at, [near, near_in, far_in, far_mate], width // groups, hidden_cols, slot_core, scale)
    return mixed, gate_step, up_step


def solution(mesh):
    in_specs = (
        P("grp", "wsh"),
        P(None, "wsh"),
        P(None, "wsh"),
        P("wsh", None),
        P("grp", None),
        P("grp", "wsh"),
        P("grp", None),
        P("grp", "wsh"),
        P("grp", "wsh"),
        P("grp", None),
        P("grp"),
    )
    out_specs = (P("grp", "wsh"), P("grp", "wsh"), P("grp", "wsh"))
    return jax.shard_map(
        per_device, mesh=mesh, in_specs=in_specs, out_specs=out_specs, check_vma=False
    )
```

```python
import math

import jax
import jax.numpy as jnp
from jax import lax
from jax.experimental import pallas as pl
from jax.experimental.pallas import tpu as pltpu
from jax.sharding import PartitionSpec as P

noise_scale = 0.5


def silu(value):
    return value / (1.0 + jnp.exp(-value))


def ring_place(index, n):
    return jnp.where(index % 2 == 0, index // 2, n - 1 - index // 2)


def ring_owner(place, n):
    place = place % n
    return jnp.where(place < n // 2, 2 * place, 2 * (n - 1 - place) + 1)


def plain_device(
    tokens,
    gate_weight,
    up_weight,
    down_weight,
    gate_left,
    gate_right,
    up_left,
    up_right,
    down_left,
    down_right,
    fitness_rank,
):
    members, width = gate_left.shape
    rows, span = tokens.shape
    per_member = rows // members
    hidden_cols = gate_weight.shape[1]
    n = lax.axis_size("wsh")
    groups = lax.axis_size("grp")
    total_members = members * groups
    hops = n // 2
    half = rows // 2
    wire = jnp.bfloat16 if n <= 8 else jnp.float32

    order = [2 * q for q in range(hops)] + [2 * (n - 1 - q) + 1 for q in range(hops, n)]
    onward = [(order[q], order[(q + 1) % n]) for q in range(n)]
    back = [(b, a) for a, b in onward]
    place = ring_place(lax.axis_index("wsh"), n)

    weight_fit = (2.0 * fitness_rank.astype(jnp.float32) - (total_members - 1)) / (
        total_members - 1
    )
    rights = jnp.concatenate([gate_right, up_right], axis=1)
    fitted = (weight_fit[:, None] * rights).astype(jnp.bfloat16)
    block = width // groups
    grp = lax.axis_index("grp")
    if groups == 4:
        pair = [(g, g ^ 2) for g in range(4)]
        mate = [(g, g ^ 1) for g in range(4)]
        lefts = jnp.stack([gate_left, up_left])
        far = (1 - grp // 2) * 2 * block
        near = (grp // 2) * 2 * block
        away = lax.dynamic_slice_in_dim(lefts, far, 2 * block, 2)
        here = lax.dynamic_slice_in_dim(lefts, near, 2 * block, 2)
        fitted_far = lax.ppermute(fitted, "grp", pair)
        left_far = lax.ppermute(away, "grp", pair)
        fitted_two = jnp.concatenate([fitted, fitted_far], axis=0)
        left_two = jnp.concatenate([here, left_far], axis=1)
        other = (1 - grp % 2) * block
        mine = (grp % 2) * block
        left_out = lax.dynamic_slice_in_dim(left_two, other, block, 2)
        left_own = lax.dynamic_slice_in_dim(left_two, mine, block, 2)
        fitted_in = lax.ppermute(fitted_two, "grp", mate)
        left_in = lax.ppermute(left_out, "grp", mate)
        fitted_all = jnp.concatenate([fitted_two, fitted_in], axis=0)
        left_all = jnp.concatenate([left_own, left_in], axis=1)
        gate_block, up_block = left_all[0], left_all[1]
    else:
        fitted_all = lax.all_gather(fitted, "grp", axis=0, tiled=True)
        gate_all = lax.all_gather(gate_left, "grp", axis=0, tiled=True)
        up_all = lax.all_gather(up_left, "grp", axis=0, tiled=True)
        gate_block = lax.dynamic_slice_in_dim(gate_all, grp * block, block, 1)
        up_block = lax.dynamic_slice_in_dim(up_all, grp * block, block, 1)
    scale = math.sqrt(width / total_members)

    def outer(left, right):
        total = lax.dot_general(
            left, right, (((0,), (0,)), ((), ())), preferred_element_type=jnp.float32
        )
        return (scale * total).astype(jnp.bfloat16)

    gate_step = outer(gate_block, fitted_all[:, :hidden_cols])
    up_step = outer(up_block, fitted_all[:, hidden_cols:])

    left_both = jnp.concatenate([gate_left, up_left], axis=0)

    def grow(total, piece, owner):
        at = owner * span
        gate_w = lax.dynamic_slice_in_dim(gate_weight, at, span, 0)
        up_w = lax.dynamic_slice_in_dim(up_weight, at, span, 0)
        left_w = lax.dynamic_slice_in_dim(left_both, at, span, 1)
        new = (
            jnp.dot(piece, gate_w, preferred_element_type=jnp.float32),
            jnp.dot(piece, up_w, preferred_element_type=jnp.float32),
            lax.dot_general(
                piece, left_w, (((1,), (1,)), ((), ())), preferred_element_type=jnp.float32
            ),
        )
        return new if total is None else tuple(a + b for a, b in zip(total, new))

    from_back, from_front = tokens, tokens
    total = None
    for hop in range(1, hops):
        sent_on, sent_back = from_back, from_front
        from_back = lax.ppermute(sent_on, "wsh", onward)
        from_front = lax.ppermute(sent_back, "wsh", back)
        if hop == 1:
            total = grow(total, tokens, ring_owner(place, n))
        else:
            total = grow(total, sent_on, ring_owner(place - hop + 1, n))
            total = grow(total, sent_back, ring_owner(place + hop - 1, n))
    top = lax.ppermute(from_back[:half], "wsh", onward)
    bottom = lax.ppermute(from_front[half:], "wsh", back)
    total = grow(total, from_back, ring_owner(place - hops + 1, n))
    total = grow(total, from_front, ring_owner(place + hops - 1, n))
    total = grow(total, jnp.concatenate([top, bottom], axis=0), ring_owner(place + hops, n))
    gate_sum, up_sum, scores = total

    own_member = (
        lax.broadcasted_iota(jnp.int32, (rows, members), 0) // per_member
        == lax.broadcasted_iota(jnp.int32, (rows, members), 1)
    )

    def pick(values):
        return jnp.sum(jnp.where(own_member, values, 0.0), axis=1)

    def spread(score, right):
        return (
            score.reshape(members, per_member)[:, :, None] * (noise_scale * right)[:, None, :]
        ).reshape(rows, right.shape[1])

    gate = gate_sum + spread(pick(scores[:, :members]), gate_right)
    up = up_sum + spread(pick(scores[:, members:]), up_right)
    hidden = (silu(gate) * up).astype(jnp.bfloat16)
    down_score = pick(
        lax.dot_general(
            hidden, down_left, (((1,), (1,)), ((), ())), preferred_element_type=jnp.float32
        )
    )

    def share(owner):
        at = owner * span
        down_w = lax.dynamic_slice_in_dim(down_weight, at, span, 1)
        right = lax.dynamic_slice_in_dim(down_right, at, span, 1)
        return jnp.dot(hidden, down_w, preferred_element_type=jnp.float32) + spread(
            down_score, right
        )

    opposite = share(ring_owner(place + hops, n)).astype(wire)
    got_on = lax.ppermute(opposite[:half], "wsh", onward)
    got_back = lax.ppermute(opposite[half:], "wsh", back)
    for hop in range(hops - 1, 0, -1):
        ahead = share(ring_owner(place + hop, n))
        behind = share(ring_owner(place - hop, n))
        if hop == hops - 1:
            ahead = jnp.concatenate([ahead[:half] + got_on.astype(jnp.float32), ahead[half:]], axis=0)
            behind = jnp.concatenate([behind[:half], behind[half:] + got_back.astype(jnp.float32)], axis=0)
        else:
            ahead = ahead + got_on.astype(jnp.float32)
            behind = behind + got_back.astype(jnp.float32)
        got_on = lax.ppermute(ahead.astype(wire), "wsh", onward)
        got_back = lax.ppermute(behind.astype(wire), "wsh", back)
    own = share(ring_owner(place, n))
    mixed = own + got_on.astype(jnp.float32) + got_back.astype(jnp.float32)
    return mixed.astype(jnp.bfloat16), gate_step, up_step


MIB = 1 << 20
VMEM = pl.BlockSpec(memory_space=pltpu.VMEM)
SMEM = pl.BlockSpec(memory_space=pltpu.SMEM)
ANY = pl.BlockSpec(memory_space=pl.ANY)
HBM = pl.BlockSpec(memory_space=pltpu.HBM)


def dims(lhs, rhs):
    return (((lhs,), (rhs,)), ((), ()))


def call(body, operands, out_shape, micros, name, in_specs=None, out_specs=None, scratch=(), limit=36, aliases=None):
    count = len(out_shape)
    return pl.pallas_call(
        body,
        out_shape=out_shape,
        in_specs=in_specs or [SMEM] + [VMEM] * (len(operands) - 1),
        out_specs=out_specs or (VMEM,) * count,
        scratch_shapes=list(scratch),
        input_output_aliases=aliases or {},
        compiler_params=pltpu.CompilerParams(vmem_limit_bytes=limit * MIB),
        cost_estimate=pl.CostEstimate(flops=int(micros * 10**9), bytes_accessed=10**6, transcendentals=0),
        name=name,
    )(*operands)


def stage_kernel(plan, count, *refs):
    sources, targets, sems = refs[:count], refs[count:-1], refs[-1]
    copies = []
    for i, (target, row) in enumerate(plan):
        height = sources[i].shape[0]
        copies.append(pltpu.make_async_copy(sources[i], targets[target].at[pl.ds(row, height)], sems.at[i]))
    for copy in copies:
        copy.start()
    for copy in copies:
        copy.wait()


def stage(groups, micros, name, earlier=()):
    arrays, plan, shapes = [], [], []
    for target, group in enumerate(groups):
        row = 0
        for array in group:
            arrays.append(pltpu.with_memory_space_constraint(array, pltpu.HBM))
            plan.append((target, row))
            row += array.shape[0]
        shapes.append(pltpu.VMEM((row, group[0].shape[1]), group[0].dtype))
    count = len(arrays)
    staged = call(
        lambda *refs: stage_kernel(plan, count, *refs[:count], *refs[count + len(earlier) :]),
        (*arrays, *earlier),
        tuple(shapes),
        micros,
        name,
        in_specs=[HBM] * count + [ANY] * len(earlier),
        scratch=[pltpu.SemaphoreType.DMA((count,))],
    )
    return [pltpu.with_memory_space_constraint(array, pltpu.VMEM) for array in staged]


def lane_block(ref, index, width, rows=slice(None), base=0):
    return ref[rows, pl.ds(pl.multiple_of(base + index * width, 128), width)]


def message_kernel(slot_far, slot_near, at, fit, rights, lefts, earlier, far, near):
    members = fit.shape[0]
    cols = rights.shape[1]
    block = lefts.shape[1] // 2
    weight = fit[...]
    gate_fit = (weight * rights[:members, :]).astype(jnp.bfloat16)
    up_fit = (weight * rights[members:, :]).astype(jnp.bfloat16)
    for out, slot in ((far, slot_far), (near, slot_near)):
        out[:, :cols] = gate_fit
        out[:, cols : 2 * cols] = up_fit
        out[:, 2 * cols : 2 * cols + block] = lane_block(lefts, at[slot], block, slice(0, members))
        out[:, 2 * cols + block :] = lane_block(lefts, at[slot], block, slice(members, 2 * members))


def messages(at, fit, rights, lefts, earlier, slot_far, slot_near):
    members = fit.shape[0]
    shape = jax.ShapeDtypeStruct((members, 2 * rights.shape[1] + lefts.shape[1]), jnp.bfloat16)
    return call(
        lambda *refs: message_kernel(slot_far, slot_near, *refs),
        (at, fit, rights, lefts, earlier),
        (shape, shape),
        2,
        "messages",
        in_specs=[SMEM] + [VMEM] * 3 + [ANY],
    )


def outer_kernel(slot, scale, at, a, b, c, d, gate_out, up_out):
    rows, cols = gate_out.shape
    parts = (a, b, c, d)
    for out, shift, right_at in ((gate_out, 0, 0), (up_out, 2 * rows, cols)):
        left = jnp.concatenate([lane_block(p, at[slot], rows, base=2 * cols + shift) for p in parts], axis=0)
        right = jnp.concatenate([p[:, right_at : right_at + cols] for p in parts], axis=0)
        total = lax.dot_general(left, right, dims(0, 0), preferred_element_type=jnp.float32)
        out[...] = (scale * total).astype(out.dtype)


def outers(at, parts, rows, cols, slot, scale):
    shape = jax.ShapeDtypeStruct((rows, cols), jnp.bfloat16)
    return call(
        lambda *refs: outer_kernel(slot, scale, *refs), (at, *parts), (shape, shape), 5, "outers"
    )


def row_block(ref, index, height):
    return ref[pl.ds(pl.multiple_of(index * height, height), height), :]


def grow_kernel(slots, first, fresh, tall, at, *refs):
    count = len(slots)
    pieces = refs[:count]
    gate_w, up_w, lefts = refs[count : count + 3]
    old = (None,) * 3 if fresh else refs[count + 3 : count + 6]
    gate, up, scores = refs[-3:]
    rows, span = pieces[0].shape
    members = scores.shape[1] // 2
    owns = [slice(at_row, at_row + members) for at_row in (first, lefts.shape[0] // 2 + first)]
    for start in range(0, rows, tall):
        part = slice(start, start + tall)
        piece = jnp.concatenate([p[part, :] for p in pieces], axis=1)
        for out, was, weight in ((gate, old[0], gate_w), (up, old[1], up_w)):
            rhs = jnp.concatenate([row_block(weight, at[s], span) for s in slots], axis=0)
            new = jnp.dot(piece, rhs, preferred_element_type=jnp.float32)
            out[part, :] = new if fresh else was[part, :] + new
        left = jnp.concatenate(
            [
                jnp.concatenate([lane_block(lefts, at[s], span, own) for s in slots], axis=1)
                for own in owns
            ],
            axis=0,
        )
        new = lax.dot_general(piece, left, dims(1, 1), preferred_element_type=jnp.float32)
        scores[part, :] = new if fresh else old[2][part, :] + new


def grow(at, pieces, slots, weights, total, first, members, micros):
    rows = pieces[0].shape[0]
    cols = weights[0].shape[1]
    count = len(pieces)
    old = () if total is None else tuple(total)
    base = 1 + count + len(weights)
    return call(
        lambda *refs: grow_kernel(slots, first, total is None, rows, *refs),
        (at, *pieces, *weights, *old),
        (
            jax.ShapeDtypeStruct((rows, cols), jnp.float32),
            jax.ShapeDtypeStruct((rows, cols), jnp.float32),
            jax.ShapeDtypeStruct((rows, 2 * members), jnp.float32),
        ),
        micros,
        "grow",
        aliases={base + i: i for i in range(len(old))},
    )


def spread_rows(score, right, per_member):
    members, cols = right.shape
    wide = jnp.broadcast_to(right[:, None, :], (members, per_member, cols))
    return score * wide.reshape(members * per_member, cols)


def finish_kernel(
    slot, first, per_member, tall, at, gate_sum, up_sum, scores, top, bottom, gate_w, up_w, lefts,
    rights, down_l, down_w, down_r, hidden_out, score_out, on_out, back_out,
):
    rows = gate_sum.shape[0]
    span = top.shape[1]
    half = rows // 2
    members = rows // per_member
    own = slice(first, first + members)
    gate_rhs, up_rhs = row_block(gate_w, at[slot], span), row_block(up_w, at[slot], span)
    group = lefts.shape[0] // 2
    own_up = slice(group + first, group + first + members)
    left = jnp.concatenate([lane_block(lefts, at[slot], span, own), lane_block(lefts, at[slot], span, own_up)], axis=0)
    down_rhs = lane_block(down_w, at[slot], span)
    down_left = down_l[own, :]
    for start in range(0, rows, tall):
        part = slice(start, start + tall)
        source, shift, out = (top, 0, on_out) if start < half else (bottom, half, back_out)
        inner = slice(start - shift, start - shift + tall)
        mine = slice(first + start // per_member, first + (start + tall) // per_member)
        mine_up = slice(group + mine.start, group + mine.stop)
        piece = source[inner, :]
        score = scores[part, :] + lax.dot_general(piece, left, dims(1, 1), preferred_element_type=jnp.float32)
        member = (lax.broadcasted_iota(jnp.int32, (tall, 2 * members), 0) + start) // per_member
        column = lax.broadcasted_iota(jnp.int32, (tall, 2 * members), 1)
        gate_score = jnp.sum(jnp.where(column == member, score, 0.0), axis=1, keepdims=True)
        up_score = jnp.sum(jnp.where(column == member + members, score, 0.0), axis=1, keepdims=True)
        gate = gate_sum[part, :] + jnp.dot(piece, gate_rhs, preferred_element_type=jnp.float32)
        up = up_sum[part, :] + jnp.dot(piece, up_rhs, preferred_element_type=jnp.float32)
        gate = gate + spread_rows(noise_scale * gate_score, rights[mine, :], per_member)
        up = up + spread_rows(noise_scale * up_score, rights[mine_up, :], per_member)
        hidden = (silu(gate) * up).astype(jnp.bfloat16)
        hidden_out[part, :] = hidden
        down = lax.dot_general(hidden, down_left, dims(1, 1), preferred_element_type=jnp.float32)
        down = jnp.where(column[:, :members] == member[:, :members], down, 0.0)
        down_score = noise_scale * jnp.sum(down, axis=1, keepdims=True)
        score_out[part, :] = jnp.broadcast_to(down_score, (tall, 128))
        share = jnp.dot(hidden, down_rhs, preferred_element_type=jnp.float32)
        share = share + spread_rows(down_score, lane_block(down_r, at[slot], span, mine), per_member)
        out[inner, :] = share.astype(out.dtype)


def finish(at, total, top, bottom, weights, others, slot, first, per_member, wire):
    rows, cols = total[0].shape
    span = top.shape[1]
    return call(
        lambda *refs: finish_kernel(slot, first, per_member, rows // 2, *refs),
        (at, *total, top, bottom, *weights, *others),
        (
            jax.ShapeDtypeStruct((rows, cols), jnp.bfloat16),
            jax.ShapeDtypeStruct((rows, 128), jnp.float32),
            jax.ShapeDtypeStruct((rows // 2, span), wire),
            jax.ShapeDtypeStruct((rows // 2, span), wire),
        ),
        4,
        "finish",
    )


def share_kernel(slots, first, per_member, at, hidden, score, down_w, down_r, *outs):
    rows = hidden.shape[0]
    own = slice(first, first + rows // per_member)
    for slot, out in zip(slots, outs):
        span = out.shape[1]
        total = jnp.dot(hidden[...], lane_block(down_w, at[slot], span), preferred_element_type=jnp.float32)
        out[...] = total + spread_rows(score[:, :1], lane_block(down_r, at[slot], span, own), per_member)


def shares(at, hidden, score, down_weight, down_right, slots, span, first, per_member, micros, passing=()):
    count = len(slots)
    shape = jax.ShapeDtypeStruct((hidden.shape[0], span), jnp.float32)
    return call(
        lambda *refs: share_kernel(slots, first, per_member, *refs[:5], *refs[5 + len(passing) :][:count]),
        (at, hidden, score, down_weight, down_right, *passing),
        (shape,) * count + tuple(jax.ShapeDtypeStruct(p.shape, p.dtype) for p in passing),
        micros,
        "shares",
        in_specs=[SMEM] + [VMEM] * 4 + [ANY] * len(passing),
        out_specs=(VMEM,) * count + (ANY,) * len(passing),
        aliases={5 + i: count + i for i in range(len(passing))},
    )


CHUNKS = 1


def per_device(
    tokens,
    gate_weight,
    up_weight,
    down_weight,
    gate_left,
    gate_right,
    up_left,
    up_right,
    down_left,
    down_right,
    fitness_rank,
):
    arguments = (tokens, gate_weight, up_weight, down_weight, gate_left, gate_right, up_left,
                 up_right, down_left, down_right, fitness_rank)
    members, width = gate_left.shape
    all_rows, span = tokens.shape
    hidden_cols = gate_weight.shape[1]
    n = lax.axis_size("wsh")
    groups = lax.axis_size("grp")
    if n != 8 or groups != 4 or span % 128 or hidden_cols % 128:
        return plain_device(*arguments)
    total_members = members * groups
    per_member = all_rows // members
    hops = n // 2
    rows = all_rows // CHUNKS
    half = rows // 2
    wire = jnp.bfloat16

    order = [2 * q for q in range(hops)] + [2 * (n - 1 - q) + 1 for q in range(hops, n)]
    onward = [(order[q], order[(q + 1) % n]) for q in range(n)]
    back = [(b, a) for a, b in onward]
    place = ring_place(lax.axis_index("wsh"), n)
    grp = lax.axis_index("grp")
    at = jnp.concatenate([
        ring_owner(place + jnp.arange(n, dtype=jnp.int32), n),
        jnp.stack([grp // 2, 1 - grp // 2, grp % 2]),
    ]).astype(jnp.int32)
    slot_near, slot_far, slot_core = n, n + 1, n + 2

    pair = [(g, g ^ 2) for g in range(4)]
    mate = [(g, g ^ 1) for g in range(4)]
    on = lambda a: lax.ppermute(a, "wsh", onward)
    back_to = lambda a: lax.ppermute(a, "wsh", back)

    weight_fit = (2.0 * fitness_rank.astype(jnp.float32) - (total_members - 1)) / (
        total_members - 1
    )
    lefts, gate_w, up_w = stage([(gate_left, up_left), (gate_weight,), (up_weight,)], 4, "stage_one")
    weights = (gate_w, up_w, lefts)

    wide = lambda a: a.astype(jnp.float32)

    def gather(piece, first):
        count = rows // per_member
        micros = 5 / CHUNKS
        a = b = piece
        total, early = None, []
        pieces, slots = [piece], [0]
        for hop in range(1, hops):
            a, b = on(a), back_to(b)
            if hop > 1:
                total = grow(at, pieces, slots, weights, total, first, count, micros)
                pieces, slots = [], []
                early.append(total[2])
            pieces, slots = pieces + [a, b], slots + [n - hop, hop]
        top, bottom = on(a[:half]), back_to(b[half:])
        total = grow(at, pieces, slots, weights, total, first, count, micros)
        return total, top, bottom, early

    def scatter(hidden, score, opposite_on, opposite_back, first, passed):
        got_on, got_back = on(opposite_on), back_to(opposite_back)
        micros = 4 / CHUNKS
        rest = []
        for hop in range(hops - 1, 0, -1):
            slots = [hop, n - hop] if hop > 1 else [hop, n - hop, 0]
            passing = (passed,) if hop == 3 else ()
            rest.append(shares(at, hidden, score, down_w, down_r, slots, span, first, per_member, micros, passing))
            ahead, behind = rest[-1][:2]
            if hop == hops - 1:
                ahead = jnp.concatenate([ahead[:half] + wide(got_on), ahead[half:]], axis=0)
                behind = jnp.concatenate([behind[:half], behind[half:] + wide(got_back)], axis=0)
            else:
                ahead = ahead + wide(got_on)
                behind = behind + wide(got_back)
            got_on, got_back = on(ahead.astype(wire)), back_to(behind.astype(wire))
        return (rest[-1][2] + wide(got_on) + wide(got_back)).astype(jnp.bfloat16), rest[-3][2]

    outs = []
    for chunk in range(CHUNKS):
        first = chunk * members // CHUNKS
        total, top, bottom, early = gather(tokens[chunk * rows : (chunk + 1) * rows], first)
        if chunk == 0:
            rights, down_l, down_r, down_w = stage(
                [(gate_right, up_right), (down_left,), (down_right,), (down_weight,)], 2, "stage_two", early[:1]
            )
            others = (rights, down_l, down_w, down_r)
            far, near = messages(at, weight_fit[:, None], rights, lefts, early[1], slot_far, slot_near)
            far_in = lax.ppermute(far, "grp", pair)
            near_in = lax.ppermute(near, "grp", mate)
        made = finish(at, total, top, bottom, weights, others, hops, first, per_member, wire)
        outs.append((made, first))
    mixed = []
    for made, first in outs:
        done, far_in = scatter(*made, first, far_in)
        mixed.append(done)
    far_mate = lax.ppermute(far_in, "grp", mate)
    mixed = mixed[0] if CHUNKS == 1 else jnp.concatenate(mixed, axis=0)
    scale = math.sqrt(width / total_members)
    gate_step, up_step = outers(at, [near, near_in, far_in, far_mate], width // groups, hidden_cols, slot_core, scale)
    return mixed, gate_step, up_step


def solution(mesh):
    in_specs = (
        P("grp", "wsh"),
        P(None, "wsh"),
        P(None, "wsh"),
        P("wsh", None),
        P("grp", None),
        P("grp", "wsh"),
        P("grp", None),
        P("grp", "wsh"),
        P("grp", "wsh"),
        P("grp", None),
        P("grp"),
    )
    out_specs = (P("grp", "wsh"), P("grp", "wsh"), P("grp", "wsh"))
    return jax.shard_map(
        per_device, mesh=mesh, in_specs=in_specs, out_specs=out_specs, check_vma=False
    )
```

```python
import math

import jax
import jax.numpy as jnp
from jax import lax
from jax.experimental import pallas as pl
from jax.experimental.pallas import tpu as pltpu
from jax.sharding import PartitionSpec as P

noise_scale = 0.5


def silu(value):
    return value / (1.0 + jnp.exp(-value))


def ring_place(index, n):
    return jnp.where(index % 2 == 0, index // 2, n - 1 - index // 2)


def ring_owner(place, n):
    place = place % n
    return jnp.where(place < n // 2, 2 * place, 2 * (n - 1 - place) + 1)


def plain_device(
    tokens,
    gate_weight,
    up_weight,
    down_weight,
    gate_left,
    gate_right,
    up_left,
    up_right,
    down_left,
    down_right,
    fitness_rank,
):
    members, width = gate_left.shape
    rows, span = tokens.shape
    per_member = rows // members
    hidden_cols = gate_weight.shape[1]
    n = lax.axis_size("wsh")
    groups = lax.axis_size("grp")
    total_members = members * groups
    hops = n // 2
    half = rows // 2
    wire = jnp.bfloat16 if n <= 8 else jnp.float32

    order = [2 * q for q in range(hops)] + [2 * (n - 1 - q) + 1 for q in range(hops, n)]
    onward = [(order[q], order[(q + 1) % n]) for q in range(n)]
    back = [(b, a) for a, b in onward]
    place = ring_place(lax.axis_index("wsh"), n)

    weight_fit = (2.0 * fitness_rank.astype(jnp.float32) - (total_members - 1)) / (
        total_members - 1
    )
    rights = jnp.concatenate([gate_right, up_right], axis=1)
    fitted = (weight_fit[:, None] * rights).astype(jnp.bfloat16)
    block = width // groups
    grp = lax.axis_index("grp")
    if groups == 4:
        pair = [(g, g ^ 2) for g in range(4)]
        mate = [(g, g ^ 1) for g in range(4)]
        lefts = jnp.stack([gate_left, up_left])
        far = (1 - grp // 2) * 2 * block
        near = (grp // 2) * 2 * block
        away = lax.dynamic_slice_in_dim(lefts, far, 2 * block, 2)
        here = lax.dynamic_slice_in_dim(lefts, near, 2 * block, 2)
        fitted_far = lax.ppermute(fitted, "grp", pair)
        left_far = lax.ppermute(away, "grp", pair)
        fitted_two = jnp.concatenate([fitted, fitted_far], axis=0)
        left_two = jnp.concatenate([here, left_far], axis=1)
        other = (1 - grp % 2) * block
        mine = (grp % 2) * block
        left_out = lax.dynamic_slice_in_dim(left_two, other, block, 2)
        left_own = lax.dynamic_slice_in_dim(left_two, mine, block, 2)
        fitted_in = lax.ppermute(fitted_two, "grp", mate)
        left_in = lax.ppermute(left_out, "grp", mate)
        fitted_all = jnp.concatenate([fitted_two, fitted_in], axis=0)
        left_all = jnp.concatenate([left_own, left_in], axis=1)
        gate_block, up_block = left_all[0], left_all[1]
    else:
        fitted_all = lax.all_gather(fitted, "grp", axis=0, tiled=True)
        gate_all = lax.all_gather(gate_left, "grp", axis=0, tiled=True)
        up_all = lax.all_gather(up_left, "grp", axis=0, tiled=True)
        gate_block = lax.dynamic_slice_in_dim(gate_all, grp * block, block, 1)
        up_block = lax.dynamic_slice_in_dim(up_all, grp * block, block, 1)
    scale = math.sqrt(width / total_members)

    def outer(left, right):
        total = lax.dot_general(
            left, right, (((0,), (0,)), ((), ())), preferred_element_type=jnp.float32
        )
        return (scale * total).astype(jnp.bfloat16)

    gate_step = outer(gate_block, fitted_all[:, :hidden_cols])
    up_step = outer(up_block, fitted_all[:, hidden_cols:])

    left_both = jnp.concatenate([gate_left, up_left], axis=0)

    def grow(total, piece, owner):
        at = owner * span
        gate_w = lax.dynamic_slice_in_dim(gate_weight, at, span, 0)
        up_w = lax.dynamic_slice_in_dim(up_weight, at, span, 0)
        left_w = lax.dynamic_slice_in_dim(left_both, at, span, 1)
        new = (
            jnp.dot(piece, gate_w, preferred_element_type=jnp.float32),
            jnp.dot(piece, up_w, preferred_element_type=jnp.float32),
            lax.dot_general(
                piece, left_w, (((1,), (1,)), ((), ())), preferred_element_type=jnp.float32
            ),
        )
        return new if total is None else tuple(a + b for a, b in zip(total, new))

    from_back, from_front = tokens, tokens
    total = None
    for hop in range(1, hops):
        sent_on, sent_back = from_back, from_front
        from_back = lax.ppermute(sent_on, "wsh", onward)
        from_front = lax.ppermute(sent_back, "wsh", back)
        if hop == 1:
            total = grow(total, tokens, ring_owner(place, n))
        else:
            total = grow(total, sent_on, ring_owner(place - hop + 1, n))
            total = grow(total, sent_back, ring_owner(place + hop - 1, n))
    top = lax.ppermute(from_back[:half], "wsh", onward)
    bottom = lax.ppermute(from_front[half:], "wsh", back)
    total = grow(total, from_back, ring_owner(place - hops + 1, n))
    total = grow(total, from_front, ring_owner(place + hops - 1, n))
    total = grow(total, jnp.concatenate([top, bottom], axis=0), ring_owner(place + hops, n))
    gate_sum, up_sum, scores = total

    own_member = (
        lax.broadcasted_iota(jnp.int32, (rows, members), 0) // per_member
        == lax.broadcasted_iota(jnp.int32, (rows, members), 1)
    )

    def pick(values):
        return jnp.sum(jnp.where(own_member, values, 0.0), axis=1)

    def spread(score, right):
        return (
            score.reshape(members, per_member)[:, :, None] * (noise_scale * right)[:, None, :]
        ).reshape(rows, right.shape[1])

    gate = gate_sum + spread(pick(scores[:, :members]), gate_right)
    up = up_sum + spread(pick(scores[:, members:]), up_right)
    hidden = (silu(gate) * up).astype(jnp.bfloat16)
    down_score = pick(
        lax.dot_general(
            hidden, down_left, (((1,), (1,)), ((), ())), preferred_element_type=jnp.float32
        )
    )

    def share(owner):
        at = owner * span
        down_w = lax.dynamic_slice_in_dim(down_weight, at, span, 1)
        right = lax.dynamic_slice_in_dim(down_right, at, span, 1)
        return jnp.dot(hidden, down_w, preferred_element_type=jnp.float32) + spread(
            down_score, right
        )

    opposite = share(ring_owner(place + hops, n)).astype(wire)
    got_on = lax.ppermute(opposite[:half], "wsh", onward)
    got_back = lax.ppermute(opposite[half:], "wsh", back)
    for hop in range(hops - 1, 0, -1):
        ahead = share(ring_owner(place + hop, n))
        behind = share(ring_owner(place - hop, n))
        if hop == hops - 1:
            ahead = jnp.concatenate([ahead[:half] + got_on.astype(jnp.float32), ahead[half:]], axis=0)
            behind = jnp.concatenate([behind[:half], behind[half:] + got_back.astype(jnp.float32)], axis=0)
        else:
            ahead = ahead + got_on.astype(jnp.float32)
            behind = behind + got_back.astype(jnp.float32)
        got_on = lax.ppermute(ahead.astype(wire), "wsh", onward)
        got_back = lax.ppermute(behind.astype(wire), "wsh", back)
    own = share(ring_owner(place, n))
    mixed = own + got_on.astype(jnp.float32) + got_back.astype(jnp.float32)
    return mixed.astype(jnp.bfloat16), gate_step, up_step


MIB = 1 << 20
VMEM = pl.BlockSpec(memory_space=pltpu.VMEM)
SMEM = pl.BlockSpec(memory_space=pltpu.SMEM)
ANY = pl.BlockSpec(memory_space=pl.ANY)
HBM = pl.BlockSpec(memory_space=pltpu.HBM)


def dims(lhs, rhs):
    return (((lhs,), (rhs,)), ((), ()))


def call(body, operands, out_shape, micros, name, in_specs=None, out_specs=None, scratch=(), limit=36, aliases=None):
    count = len(out_shape)
    return pl.pallas_call(
        body,
        out_shape=out_shape,
        in_specs=in_specs or [SMEM] + [VMEM] * (len(operands) - 1),
        out_specs=out_specs or (VMEM,) * count,
        scratch_shapes=list(scratch),
        input_output_aliases=aliases or {},
        compiler_params=pltpu.CompilerParams(vmem_limit_bytes=limit * MIB),
        cost_estimate=pl.CostEstimate(flops=int(micros * 10**9), bytes_accessed=10**6, transcendentals=0),
        name=name,
    )(*operands)


def stage_kernel(plan, count, *refs):
    sources, targets, sems = refs[:count], refs[count:-1], refs[-1]
    copies = []
    for i, (target, row) in enumerate(plan):
        height = sources[i].shape[0]
        copies.append(pltpu.make_async_copy(sources[i], targets[target].at[pl.ds(row, height)], sems.at[i]))
    for copy in copies:
        copy.start()
    for copy in copies:
        copy.wait()


def stage(groups, micros, name, earlier=()):
    arrays, plan, shapes = [], [], []
    for target, group in enumerate(groups):
        row = 0
        for array in group:
            arrays.append(pltpu.with_memory_space_constraint(array, pltpu.HBM))
            plan.append((target, row))
            row += array.shape[0]
        shapes.append(pltpu.VMEM((row, group[0].shape[1]), group[0].dtype))
    count = len(arrays)
    staged = call(
        lambda *refs: stage_kernel(plan, count, *refs[:count], *refs[count + len(earlier) :]),
        (*arrays, *earlier),
        tuple(shapes),
        micros,
        name,
        in_specs=[HBM] * count + [ANY] * len(earlier),
        scratch=[pltpu.SemaphoreType.DMA((count,))],
    )
    return [pltpu.with_memory_space_constraint(array, pltpu.VMEM) for array in staged]


def lane_block(ref, index, width, rows=slice(None), base=0):
    return ref[rows, pl.ds(pl.multiple_of(base + index * width, 128), width)]


def message_kernel(slot_far, slot_near, at, fit, rights, lefts, earlier, far, near):
    members = fit.shape[0]
    cols = rights.shape[1]
    block = lefts.shape[1] // 2
    weight = fit[...]
    gate_fit = (weight * rights[:members, :]).astype(jnp.bfloat16)
    up_fit = (weight * rights[members:, :]).astype(jnp.bfloat16)
    for out, slot in ((far, slot_far), (near, slot_near)):
        out[:, :cols] = gate_fit
        out[:, cols : 2 * cols] = up_fit
        out[:, 2 * cols : 2 * cols + block] = lane_block(lefts, at[slot], block, slice(0, members))
        out[:, 2 * cols + block :] = lane_block(lefts, at[slot], block, slice(members, 2 * members))


def messages(at, fit, rights, lefts, earlier, slot_far, slot_near):
    members = fit.shape[0]
    shape = jax.ShapeDtypeStruct((members, 2 * rights.shape[1] + lefts.shape[1]), jnp.bfloat16)
    return call(
        lambda *refs: message_kernel(slot_far, slot_near, *refs),
        (at, fit, rights, lefts, earlier),
        (shape, shape),
        2,
        "messages",
        in_specs=[SMEM] + [VMEM] * 3 + [ANY],
    )


def outer_kernel(slot, scale, at, a, b, c, d, gate_out, up_out):
    rows, cols = gate_out.shape
    parts = (a, b, c, d)
    for out, shift, right_at in ((gate_out, 0, 0), (up_out, 2 * rows, cols)):
        left = jnp.concatenate([lane_block(p, at[slot], rows, base=2 * cols + shift) for p in parts], axis=0)
        right = jnp.concatenate([p[:, right_at : right_at + cols] for p in parts], axis=0)
        total = lax.dot_general(left, right, dims(0, 0), preferred_element_type=jnp.float32)
        out[...] = (scale * total).astype(out.dtype)


def outers(at, parts, rows, cols, slot, scale):
    shape = jax.ShapeDtypeStruct((rows, cols), jnp.bfloat16)
    return call(
        lambda *refs: outer_kernel(slot, scale, *refs), (at, *parts), (shape, shape), 5, "outers"
    )


def row_block(ref, index, height):
    return ref[pl.ds(pl.multiple_of(index * height, height), height), :]


def grow_kernel(slots, first, fresh, tall, at, *refs):
    count = len(slots)
    pieces = refs[:count]
    gate_w, up_w, lefts = refs[count : count + 3]
    old = (None,) * 3 if fresh else refs[count + 3 : count + 6]
    gate, up, scores = refs[-3:]
    rows, span = pieces[0].shape
    members = scores.shape[1] // 2
    owns = [slice(at_row, at_row + members) for at_row in (first, lefts.shape[0] // 2 + first)]
    for start in range(0, rows, tall):
        part = slice(start, start + tall)
        piece = jnp.concatenate([p[part, :] for p in pieces], axis=1)
        for out, was, weight in ((gate, old[0], gate_w), (up, old[1], up_w)):
            rhs = jnp.concatenate([row_block(weight, at[s], span) for s in slots], axis=0)
            new = jnp.dot(piece, rhs, preferred_element_type=jnp.float32)
            out[part, :] = new if fresh else was[part, :] + new
        left = jnp.concatenate(
            [
                jnp.concatenate([lane_block(lefts, at[s], span, own) for s in slots], axis=1)
                for own in owns
            ],
            axis=0,
        )
        new = lax.dot_general(piece, left, dims(1, 1), preferred_element_type=jnp.float32)
        scores[part, :] = new if fresh else old[2][part, :] + new


def grow(at, pieces, slots, weights, total, first, members, micros):
    rows = pieces[0].shape[0]
    cols = weights[0].shape[1]
    count = len(pieces)
    old = () if total is None else tuple(total)
    base = 1 + count + len(weights)
    return call(
        lambda *refs: grow_kernel(slots, first, total is None, rows, *refs),
        (at, *pieces, *weights, *old),
        (
            jax.ShapeDtypeStruct((rows, cols), jnp.float32),
            jax.ShapeDtypeStruct((rows, cols), jnp.float32),
            jax.ShapeDtypeStruct((rows, 2 * members), jnp.float32),
        ),
        micros,
        "grow",
        aliases={base + i: i for i in range(len(old))},
    )


def spread_rows(score, right, per_member):
    members, cols = right.shape
    wide = jnp.broadcast_to(right[:, None, :], (members, per_member, cols))
    return score * wide.reshape(members * per_member, cols)


def finish_kernel(
    slot, first, per_member, wide, at, gate_sum, up_sum, scores, top, bottom, gate_w, up_w, lefts,
    rights, down_l, down_w, down_r, hidden_out, score_out, on_out, back_out,
):
    rows = gate_sum.shape[0]
    span = top.shape[1]
    half = rows // 2
    members = rows // per_member
    own = slice(first, first + members)
    cols = gate_sum.shape[1]
    weight_rows = pl.ds(pl.multiple_of(at[slot] * span, span), span)
    group = lefts.shape[0] // 2
    own_up = slice(group + first, group + first + members)
    left = jnp.concatenate([lane_block(lefts, at[slot], span, own), lane_block(lefts, at[slot], span, own_up)], axis=0)
    down_rhs = lane_block(down_w, at[slot], span)
    down_left = down_l[own, :]
    piece = jnp.concatenate([top[...], bottom[...]], axis=0)
    score = scores[...] + lax.dot_general(piece, left, dims(1, 1), preferred_element_type=jnp.float32)
    member = lax.broadcasted_iota(jnp.int32, (rows, 2 * members), 0) // per_member
    column = lax.broadcasted_iota(jnp.int32, (rows, 2 * members), 1)
    gate_score = noise_scale * jnp.sum(jnp.where(column == member, score, 0.0), axis=1, keepdims=True)
    up_score = noise_scale * jnp.sum(jnp.where(column == member + members, score, 0.0), axis=1, keepdims=True)
    for at_col in range(0, cols, wide):
        some = slice(at_col, at_col + wide)
        rhs = jnp.concatenate([gate_w[weight_rows, some], up_w[weight_rows, some]], axis=1)
        both = jnp.dot(piece, rhs, preferred_element_type=jnp.float32)
        gate = gate_sum[:, some] + both[:, :wide] + spread_rows(gate_score, rights[own, some], per_member)
        up = up_sum[:, some] + both[:, wide:] + spread_rows(up_score, rights[own_up, some], per_member)
        hidden_out[:, some] = (silu(gate) * up).astype(jnp.bfloat16)
    hidden = hidden_out[...]
    down = lax.dot_general(hidden, down_left, dims(1, 1), preferred_element_type=jnp.float32)
    down = jnp.where(column[:, :members] == member[:, :members], down, 0.0)
    down_score = noise_scale * jnp.sum(down, axis=1, keepdims=True)
    score_out[...] = jnp.broadcast_to(down_score, (rows, 128))
    share = jnp.dot(hidden, down_rhs, preferred_element_type=jnp.float32)
    share = (share + spread_rows(down_score, lane_block(down_r, at[slot], span, own), per_member)).astype(on_out.dtype)
    on_out[...] = share[:half, :]
    back_out[...] = share[half:, :]


def finish(at, total, top, bottom, weights, others, slot, first, per_member, wire):
    rows, cols = total[0].shape
    span = top.shape[1]
    return call(
        lambda *refs: finish_kernel(slot, first, per_member, 128, *refs),
        (at, *total, top, bottom, *weights, *others),
        (
            jax.ShapeDtypeStruct((rows, cols), jnp.bfloat16),
            jax.ShapeDtypeStruct((rows, 128), jnp.float32),
            jax.ShapeDtypeStruct((rows // 2, span), wire),
            jax.ShapeDtypeStruct((rows // 2, span), wire),
        ),
        4,
        "finish",
    )


def share_kernel(slots, first, per_member, at, hidden, score, down_w, down_r, *outs):
    rows = hidden.shape[0]
    own = slice(first, first + rows // per_member)
    for slot, out in zip(slots, outs):
        span = out.shape[1]
        total = jnp.dot(hidden[...], lane_block(down_w, at[slot], span), preferred_element_type=jnp.float32)
        out[...] = total + spread_rows(score[:, :1], lane_block(down_r, at[slot], span, own), per_member)


def shares(at, hidden, score, down_weight, down_right, slots, span, first, per_member, micros, passing=()):
    count = len(slots)
    shape = jax.ShapeDtypeStruct((hidden.shape[0], span), jnp.float32)
    return call(
        lambda *refs: share_kernel(slots, first, per_member, *refs[:5], *refs[5 + len(passing) :][:count]),
        (at, hidden, score, down_weight, down_right, *passing),
        (shape,) * count + tuple(jax.ShapeDtypeStruct(p.shape, p.dtype) for p in passing),
        micros,
        "shares",
        in_specs=[SMEM] + [VMEM] * 4 + [ANY] * len(passing),
        out_specs=(VMEM,) * count + (ANY,) * len(passing),
        aliases={5 + i: count + i for i in range(len(passing))},
    )


CHUNKS = 1


def per_device(
    tokens,
    gate_weight,
    up_weight,
    down_weight,
    gate_left,
    gate_right,
    up_left,
    up_right,
    down_left,
    down_right,
    fitness_rank,
):
    arguments = (tokens, gate_weight, up_weight, down_weight, gate_left, gate_right, up_left,
                 up_right, down_left, down_right, fitness_rank)
    members, width = gate_left.shape
    all_rows, span = tokens.shape
    hidden_cols = gate_weight.shape[1]
    n = lax.axis_size("wsh")
    groups = lax.axis_size("grp")
    if n != 8 or groups != 4 or span % 128 or hidden_cols % 128:
        return plain_device(*arguments)
    total_members = members * groups
    per_member = all_rows // members
    hops = n // 2
    rows = all_rows // CHUNKS
    half = rows // 2
    wire = jnp.bfloat16

    order = [2 * q for q in range(hops)] + [2 * (n - 1 - q) + 1 for q in range(hops, n)]
    onward = [(order[q], order[(q + 1) % n]) for q in range(n)]
    back = [(b, a) for a, b in onward]
    place = ring_place(lax.axis_index("wsh"), n)
    grp = lax.axis_index("grp")
    at = jnp.concatenate([
        ring_owner(place + jnp.arange(n, dtype=jnp.int32), n),
        jnp.stack([grp // 2, 1 - grp // 2, grp % 2]),
    ]).astype(jnp.int32)
    slot_near, slot_far, slot_core = n, n + 1, n + 2

    pair = [(g, g ^ 2) for g in range(4)]
    mate = [(g, g ^ 1) for g in range(4)]
    on = lambda a: lax.ppermute(a, "wsh", onward)
    back_to = lambda a: lax.ppermute(a, "wsh", back)

    weight_fit = (2.0 * fitness_rank.astype(jnp.float32) - (total_members - 1)) / (
        total_members - 1
    )
    lefts, gate_w, up_w = stage([(gate_left, up_left), (gate_weight,), (up_weight,)], 4, "stage_one")
    weights = (gate_w, up_w, lefts)

    wide = lambda a: a.astype(jnp.float32)

    def gather(piece, first):
        count = rows // per_member
        micros = 5 / CHUNKS
        a = b = piece
        total, early = None, []
        pieces, slots = [piece], [0]
        for hop in range(1, hops):
            a, b = on(a), back_to(b)
            if hop > 1:
                total = grow(at, pieces, slots, weights, total, first, count, micros)
                pieces, slots = [], []
                early.append(total[2])
            pieces, slots = pieces + [a, b], slots + [n - hop, hop]
        top, bottom = on(a[:half]), back_to(b[half:])
        total = grow(at, pieces, slots, weights, total, first, count, micros)
        return total, top, bottom, early

    def scatter(hidden, score, opposite_on, opposite_back, first, passed):
        got_on, got_back = on(opposite_on), back_to(opposite_back)
        micros = 4 / CHUNKS
        rest = []
        for hop in range(hops - 1, 0, -1):
            slots = [hop, n - hop] if hop > 1 else [hop, n - hop, 0]
            passing = (passed,) if hop == 3 else ()
            rest.append(shares(at, hidden, score, down_w, down_r, slots, span, first, per_member, micros, passing))
            ahead, behind = rest[-1][:2]
            if hop == hops - 1:
                ahead = jnp.concatenate([ahead[:half] + wide(got_on), ahead[half:]], axis=0)
                behind = jnp.concatenate([behind[:half], behind[half:] + wide(got_back)], axis=0)
            else:
                ahead = ahead + wide(got_on)
                behind = behind + wide(got_back)
            got_on, got_back = on(ahead.astype(wire)), back_to(behind.astype(wire))
        return (rest[-1][2] + wide(got_on) + wide(got_back)).astype(jnp.bfloat16), rest[-3][2]

    outs = []
    for chunk in range(CHUNKS):
        first = chunk * members // CHUNKS
        total, top, bottom, early = gather(tokens[chunk * rows : (chunk + 1) * rows], first)
        if chunk == 0:
            rights, down_l, down_r, down_w = stage(
                [(gate_right, up_right), (down_left,), (down_right,), (down_weight,)], 2, "stage_two", early[:1]
            )
            others = (rights, down_l, down_w, down_r)
            far, near = messages(at, weight_fit[:, None], rights, lefts, early[1], slot_far, slot_near)
            far_in = lax.ppermute(far, "grp", pair)
            near_in = lax.ppermute(near, "grp", mate)
        made = finish(at, total, top, bottom, weights, others, hops, first, per_member, wire)
        outs.append((made, first))
    mixed = []
    for made, first in outs:
        done, far_in = scatter(*made, first, far_in)
        mixed.append(done)
    far_mate = lax.ppermute(far_in, "grp", mate)
    mixed = mixed[0] if CHUNKS == 1 else jnp.concatenate(mixed, axis=0)
    scale = math.sqrt(width / total_members)
    gate_step, up_step = outers(at, [near, near_in, far_in, far_mate], width // groups, hidden_cols, slot_core, scale)
    return mixed, gate_step, up_step


def solution(mesh):
    in_specs = (
        P("grp", "wsh"),
        P(None, "wsh"),
        P(None, "wsh"),
        P("wsh", None),
        P("grp", None),
        P("grp", "wsh"),
        P("grp", None),
        P("grp", "wsh"),
        P("grp", "wsh"),
        P("grp", None),
        P("grp"),
    )
    out_specs = (P("grp", "wsh"), P("grp", "wsh"), P("grp", "wsh"))
    return jax.shard_map(
        per_device, mesh=mesh, in_specs=in_specs, out_specs=out_specs, check_vma=False
    )
```
